256 devices in a mesh: row: 8 (over x, y_hi), col: 4 (over y_lo, core), dp: 8 (over z).
Axes of the slice: x: 4, y: 4 (y_hi: 2, y_lo: 2; y = y_hi * 2 + y_lo), z: 8, core: 2. Of those that a mesh axis runs over, the one named last changes fastest.
Arguments:
- qkv: bfloat16 [8, 192, 96, 3072], P('dp', 'row', 'col'), may hold values from -64 to 64, as said below
- grad_out: bfloat16 [8, 192, 96, 1024], P('dp', 'row', 'col'), may hold values from -6 to 6
- w_qkv: bfloat16 [1024, 3072], P('dp'), may hold values from -0.1875 to 0.1875
- w_proj: bfloat16 [1024, 1024], replicated, may hold values from -0.1875 to 0.1875
- norm_gain: float32 [1024], replicated, may hold values from 0.5 to 1.5
- region: int32 [192, 96], P('row', 'col'), may hold values from 0 to 3
Outputs:
- grad_in: bfloat16 [8, 192, 96, 1024], P('dp', 'row', 'col')
- grad_proj: float32 [1024, 1024], P(('row', 'col', 'dp'))
- grad_gain: float32 [1024], replicated
The draws below stay inside these ranges and needn't reach their ends.
Inputs may be any that keep to these rules, and one draw needn't show every extreme that they name: `qkv`: entries of the saved projections are finite reals.
All inputs are finite; a program needn't handle non-finite values.
Results may differ from the reference program's by a relative error of at most 0.013.
Values may be sent and summed in bfloat16 or wider, within the bound.
No kernel may reach another device: no remote copies, remote signals or barrier semaphores. Data moves between devices by JAX's collectives and lax.ppermute only.
A program may use at most 128 MiB of HBM per device.

```python
import jax
import jax.numpy as jnp
from jax import lax

C = 1024
HEADS = 32
WIN = 24
BATCH = 8
NH = 192
NW = 96


def draw_qkv(key, part):
    key = jax.random.fold_in(key, 11)
    first = jax.random.fold_in(key, 0)
    base = jnp.clip(jax.random.normal(first, (BATCH, NH, NW, 3 * C), jnp.float32), -4.0, 4.0)
    return base.astype(jnp.bfloat16)


def touch_ends(values, stream_key, smallest, largest):
    index_at = [jax.random.randint(jax.random.fold_in(stream_key, axis), (), 0, length) for axis, length in enumerate(values.shape)]
    longest = values.shape.index(max(values.shape))
    beside = index_at[:longest] + [(index_at[longest] + 1) % values.shape[longest]] + index_at[longest + 1:]
    return values.at[tuple(index_at)].set(smallest).at[tuple(beside)].set(largest)


def shard_levels(key, shape, pieces, least, top_value):
    def one(dim, blocks):
        steps = jax.random.uniform(jax.random.fold_in(jax.random.fold_in(key, 6), dim), (blocks,), jnp.float32, least / len(pieces), top_value / len(pieces))
        return jnp.repeat(jnp.exp(steps), shape[dim] // blocks).reshape((-1,) + (1,) * (len(shape) - dim - 1))

    level = one(*pieces[0])
    for cut in pieces[1:]:
        level = level * one(*cut)
    return level


def noise(stream_key, extent, scale, bound, cuts=(), held_as=jnp.bfloat16):
    factor_of = shard_levels(stream_key, extent, cuts, -0.22, 0.18) if cuts else 1.0
    entries = jax.random.normal(stream_key, extent, jnp.float32) * scale * factor_of
    return jnp.minimum(jnp.maximum(entries, -bound), bound).astype(held_as)


def setup_inputs(seed: int = 0) -> dict:
    seeds = jax.random.split(jax.random.key(seed), 7)
    qkv = draw_qkv(jax.random.fold_in(seeds[6], 71), 0)
    grad_out = noise(seeds[1], (BATCH, NH, NW, C), 1.0, 6.0, ((0, 8), (1, 8), (2, 4)))
    w_qkv = noise(seeds[2], (C, 3 * C), C ** -0.5, 0.1875, ((0, 8),))
    w_proj = noise(seeds[3], (C, C), C ** -0.5, 0.1875)
    norm_gain = jnp.clip(1.0 + 0.1 * jax.random.normal(seeds[4], (C,), jnp.float32), 0.5, 1.5)
    region = touch_ends(jax.random.randint(seeds[5], (NH, NW), 0, 4), jax.random.fold_in(seeds[5], 1), 0, 3).astype(jnp.int32)
    return dict(qkv=qkv, grad_out=grad_out, w_qkv=w_qkv, w_proj=w_proj, norm_gain=norm_gain, region=region)


def softmax_rows(query, keys, same, scale):
    scores = jnp.einsum('qhd,khd->hqk', query.astype(jnp.float32), keys.astype(jnp.float32)) * scale
    scores = jnp.where(same[None], scores, -1e+30)
    top = lax.optimization_barrier(jnp.max(scores, axis=-1, keepdims=True))
    expo = jnp.where(same[None], jnp.exp(scores - top), 0.0)
    return expo / lax.optimization_barrier(jnp.sum(expo, axis=-1, keepdims=True))

def split_groups(values, heads):
    tokens, width = values.shape
    return values.reshape(tokens, heads // 8, 8, width // heads).transpose(1, 0, 2, 3)

def join_groups(values):
    return values.transpose(1, 0, 2, 3).reshape(values.shape[1], -1)

def window_grads(qkv_t, dz, region_t, w_proj, gain):
    width = w_proj.shape[0]
    scale = (width // HEADS) ** (-0.5)
    same = region_t[:, None] == region_t[None, :]
    query = split_groups(qkv_t[:, :width], HEADS)
    keys = split_groups(qkv_t[:, width:2 * width], HEADS)
    values = split_groups(qkv_t[:, 2 * width:], HEADS)

    def forward(parts):
        probs = softmax_rows(parts[0], parts[1], same, scale).astype(jnp.bfloat16)
        return jnp.einsum('hqk,khd->qhd', probs.astype(jnp.float32), parts[2].astype(jnp.float32))
    attn = join_groups(lax.map(forward, (query, keys, values))).astype(jnp.bfloat16)
    proj = jnp.dot(attn, w_proj, preferred_element_type=jnp.float32)
    centred = proj - lax.optimization_barrier(jnp.mean(proj, axis=-1, keepdims=True))
    rstd = lax.rsqrt(lax.optimization_barrier(jnp.mean(centred * centred, axis=-1, keepdims=True)) + 1e-05)
    normed = centred * rstd
    gain_term = lax.optimization_barrier(jnp.sum(dz * normed, axis=0))
    scaled = dz * gain
    dproj = rstd * (scaled - lax.optimization_barrier(jnp.mean(scaled, axis=-1, keepdims=True)) - normed * lax.optimization_barrier(jnp.mean(scaled * normed, axis=-1, keepdims=True)))
    dproj = dproj.astype(jnp.bfloat16)
    dattn = jnp.dot(dproj, w_proj.T, preferred_element_type=jnp.float32).astype(jnp.bfloat16)
    dgroups = split_groups(dattn, HEADS)

    def backward(parts):
        q_f = parts[0].astype(jnp.float32)
        k_f = parts[1].astype(jnp.float32)
        v_f = parts[2].astype(jnp.float32)
        do_f = parts[3].astype(jnp.float32)
        probs = softmax_rows(parts[0], parts[1], same, scale)
        probs_low = probs.astype(jnp.bfloat16).astype(jnp.float32)
        dprobs = jnp.einsum('qhd,khd->hqk', do_f, v_f)
        delta = lax.optimization_barrier(jnp.sum(probs * dprobs, axis=-1, keepdims=True))
        dscores = (probs * (dprobs - delta) * scale).astype(jnp.bfloat16).astype(jnp.float32)
        dq = jnp.einsum('hqk,khd->qhd', dscores, k_f)
        dk = jnp.einsum('hqk,qhd->khd', dscores, q_f)
        dv = jnp.einsum('hqk,qhd->khd', probs_low, do_f)
        return (dq, dk, dv)
    dq, dk, dv = lax.map(backward, (query, keys, values, dgroups))
    dqkv = jnp.concatenate([join_groups(dq), join_groups(dk), join_groups(dv)], axis=1).astype(jnp.bfloat16)
    return (attn, dproj, dqkv, gain_term)

def to_windows(values):
    batch, rows, cols, width = values.shape
    blocks = values.reshape(batch, rows // WIN, WIN, cols // WIN, WIN, width)
    return blocks.transpose(0, 1, 3, 2, 4, 5).reshape(-1, WIN * WIN, width)

def from_windows(values, batch, rows, cols):
    width = values.shape[-1]
    blocks = values.reshape(batch, rows // WIN, cols // WIN, WIN, WIN, width)
    return blocks.transpose(0, 1, 3, 2, 4, 5).reshape(batch, rows, cols, width)

def reference(qkv, grad_out, w_qkv, w_proj, norm_gain, region):
    shift = WIN // 2
    rolled = jnp.roll(grad_out, (-shift, -shift), axis=(1, 2)).astype(jnp.float32)
    regions = jnp.broadcast_to(region[None, :, :, None], (BATCH, NH, NW, 1)).astype(jnp.int32)

    def one(parts):
        return window_grads(parts[0], parts[1], parts[2][:, 0], w_proj, norm_gain)
    attn, dproj, dqkv, gain_terms = lax.map(one, (to_windows(qkv), to_windows(rolled), to_windows(regions)))
    norm = (BATCH * NH * NW) ** (-0.5)
    grad_gain = lax.optimization_barrier(jnp.sum(gain_terms, axis=0)) * norm
    grad_proj = lax.dot_general(attn.reshape(-1, C), dproj.reshape(-1, C), (((0,), (0,)), ((), ())), preferred_element_type=jnp.float32) * norm
    back = jnp.dot(dqkv.reshape(-1, 3 * C), w_qkv.T, preferred_element_type=jnp.float32).astype(jnp.bfloat16)
    back = from_windows(back, BATCH, NH, NW)
    back = jnp.roll(back, (shift, shift), axis=(1, 2))
    grad_in = (grad_out.astype(jnp.float32) + back.astype(jnp.float32)).astype(jnp.bfloat16)
    return (grad_in, grad_proj, grad_gain)
```

```python
import math

import jax
import jax.numpy as jnp
from jax import lax
from jax.experimental import pallas as pl
from jax.experimental.pallas import tpu as pltpu
from jax.sharding import PartitionSpec as P

HEADS = 32
GROUP = 4
BF = jnp.bfloat16
F32 = jnp.float32
NT = (((1,), (1,)), ((), ()))
TN = (((0,), (0,)), ((), ()))
LIMIT = 56 * 2**20
GAIN_ROWS = 16
STEPS = (
    ("col", 1), ("col", 2), ("row", 2), ("row", 4), ("row", 1), ("dp", 4), ("dp", 2), ("dp", 1),
)


def params():
    return pltpu.CompilerParams(vmem_limit_bytes=LIMIT)


def shape(*dims):
    return lambda kind: jax.ShapeDtypeStruct(dims, kind)


def split3(value):
    high = value.astype(BF)
    rest = value - high.astype(F32)
    mid = rest.astype(BF)
    return high, mid, (rest - mid.astype(F32)).astype(BF)


def forward_kernel(q_ref, k_ref, v_ref, hot_ref, mask_ref, p_ref, o_ref, inv_ref):
    tokens, lanes = q_ref.shape
    factor = (lanes // GROUP) ** (-0.5) * math.log2(math.e)
    keys, values = k_ref[...], v_ref[...]
    head = lax.broadcasted_iota(jnp.int32, (tokens, lanes), 1) // (lanes // GROUP)
    left = jnp.concatenate([q_ref[...], hot_ref[...]], axis=1)
    summed = jnp.concatenate([values, jnp.ones_like(values)], axis=1)
    out, inverse = None, None
    for h in range(GROUP):
        own = jnp.where(head == h, keys, jnp.zeros_like(keys))
        right = jnp.concatenate([own, mask_ref[...]], axis=1)
        scores = lax.dot_general(left, right, NT, preferred_element_type=F32)
        top = jnp.max(scores, axis=1, keepdims=True)
        expo = jnp.exp2((scores - top) * factor).astype(BF)
        p_ref[h] = expo
        both = jnp.dot(expo, summed, preferred_element_type=F32)
        inv = 1.0 / both[:, lanes:]
        attn = both[:, :lanes] * inv
        out = attn if out is None else jnp.where(head == h, attn, out)
        inverse = inv if inverse is None else jnp.where(head == h, inv, inverse)
    o_ref[...] = out
    inv_ref[...] = inverse


def backward_kernel(p_ref, q_ref, k_ref, v_ref, do_ref, o_ref, inv_ref, dq_ref, dk_ref, dv_ref):
    tokens, lanes = q_ref.shape
    size = lanes // GROUP
    scale = size ** (-0.5)
    keys, values, dout, inv = k_ref[...], v_ref[...], do_ref[...], inv_ref[...]
    lane = lax.broadcasted_iota(jnp.int32, (tokens, lanes), 1)
    head = lane // size
    dout_f = dout.astype(F32)
    row_i = lax.broadcasted_iota(jnp.int32, (lanes, lanes), 0) // size
    col_i = lax.broadcasted_iota(jnp.int32, (lanes, lanes), 1) // 4
    pick = jnp.where(row_i == col_i, 1.0, 0.0).astype(BF)
    parts = jnp.concatenate(split3(dout_f * o_ref[...]), axis=1)
    delta = jnp.dot(parts, jnp.concatenate([pick] * 3, axis=0), preferred_element_type=F32)
    d_high = delta.astype(BF).astype(F32)
    d_rest = delta - d_high
    d_mid = d_rest.astype(BF).astype(F32)
    which = lane % 4
    columns = jnp.where(
        which == 0, d_high, jnp.where(which == 1, d_mid, jnp.where(which == 2, d_rest - d_mid, 0.0))
    ).astype(BF)
    left = jnp.concatenate([dout, columns], axis=1)
    dout_t = (dout_f * inv).T.astype(BF)
    query_t = (q_ref[...].astype(F32) * (inv * scale)).T.astype(BF)
    dq, dks, dvs = None, [], []
    for h in range(GROUP):
        probs = p_ref[h]
        own = jnp.where(head == h, values, jnp.zeros_like(values))
        minus = jnp.where(lane // 4 == h, -1.0, 0.0).astype(BF)
        right = jnp.concatenate([own, minus], axis=1)
        dprobs = lax.dot_general(left, right, NT, preferred_element_type=F32)
        dscores = (probs.astype(F32) * dprobs).astype(BF)
        part = jnp.dot(dscores, keys, preferred_element_type=F32)
        dq = part if dq is None else jnp.where(head == h, part, dq)
        rows = slice(size * h, size * (h + 1))
        dks.append(jnp.dot(query_t[rows], dscores, preferred_element_type=F32))
        dvs.append(jnp.dot(dout_t[rows], probs, preferred_element_type=F32))
    dq_ref[...] = (dq * (inv * scale)).astype(BF)
    dk_ref[...] = jnp.concatenate(dks, axis=0).T.astype(BF)
    dv_ref[...] = jnp.concatenate(dvs, axis=0).T.astype(BF)


def column_block(tokens, offset):
    return pl.BlockSpec((tokens, 128), lambda g: (0, g + offset))


def forward(qkv, hot, mask, first, count):
    tokens = qkv.shape[0]
    per = qkv.shape[1] // 3 // 128
    whole = pl.BlockSpec((tokens, 128), lambda g: (0, 0))
    out = shape(tokens, count * 128)(F32)
    return pl.pallas_call(
        forward_kernel,
        grid=(count,),
        in_specs=[column_block(tokens, first + per * i) for i in range(3)] + [whole, whole],
        out_specs=[pl.BlockSpec((GROUP, tokens, tokens), lambda g: (g, 0, 0))]
        + [column_block(tokens, 0)] * 2,
        out_shape=[shape(count * GROUP, tokens, tokens)(BF), out, out],
        compiler_params=params(),
        cost_estimate=pl.CostEstimate(
            flops=count * 3_200_000_000, bytes_accessed=count * 4_000_000, transcendentals=0
        ),
        name="attn_forward",
    )(qkv, qkv, qkv, hot, mask)


def backward(probs, qkv, dattn, out, inverse, first, count):
    tokens = qkv.shape[0]
    per = qkv.shape[1] // 3 // 128
    return pl.pallas_call(
        backward_kernel,
        grid=(count,),
        in_specs=[pl.BlockSpec((GROUP, tokens, tokens), lambda g: (g, 0, 0))]
        + [column_block(tokens, first + per * i) for i in range(3)]
        + [column_block(tokens, first)]
        + [column_block(tokens, 0)] * 2,
        out_specs=[column_block(tokens, 0)] * 3,
        out_shape=[shape(tokens, count * 128)(BF)] * 3,
        compiler_params=params(),
        cost_estimate=pl.CostEstimate(
            flops=count * 3_600_000_000, bytes_accessed=count * 4_000_000, transcendentals=0
        ),
        name="attn_backward",
    )(probs, qkv, qkv, qkv, dattn, out, inverse)


def split_gain(value):
    high = value.astype(BF)
    low = (value - high.astype(F32)).astype(BF)
    held = high.astype(F32) + low.astype(F32)
    rows = lax.broadcasted_iota(jnp.int32, (GAIN_ROWS, value.shape[1]), 0)
    packed = jnp.where(rows == 0, high.astype(F32), jnp.where(rows == 1, low.astype(F32), 0.0))
    return packed.astype(BF), held


def hand_out(bit, low, high, gain, send_ref, keep_ref, gain_ref):
    packed, held = split_gain(gain)
    send_ref[0:GAIN_ROWS] = packed
    send_ref[GAIN_ROWS:] = jnp.where(bit, low, high).astype(BF)
    keep_ref[...] = jnp.where(bit, high, low)
    gain_ref[...] = held


def middle_kernel(order, bit_ref, *refs):
    outs, (w_ref, dz_ref, gain_ref, do_ref, send_ref, keep_ref, term_ref, sums) = refs[:-8], refs[-8:]
    attn = jnp.concatenate([ref[...].astype(BF) for ref in outs], axis=1)
    weights = w_ref[...]
    proj = jnp.dot(attn, weights, preferred_element_type=F32)
    centred = proj - jnp.mean(proj, axis=1, keepdims=True)
    rstd = lax.rsqrt(jnp.mean(centred * centred, axis=1, keepdims=True) + 1e-05)
    normed = centred * rstd
    dz = dz_ref[...].astype(F32)
    term = jnp.sum(dz * normed, axis=0, keepdims=True)
    scaled = dz * gain_ref[...]
    mean = jnp.mean(scaled, axis=1, keepdims=True)
    dot = jnp.mean(scaled * normed, axis=1, keepdims=True)
    dproj = (rstd * (scaled - mean - normed * dot)).astype(BF)
    do_ref[...] = lax.dot_general(dproj, weights, NT, preferred_element_type=F32).astype(BF)
    sums[...] = lax.dot_general(attn, dproj, TN, preferred_element_type=F32)
    half = len(order) // 2
    size = sums.shape[0] // len(order)
    low, high = (
        jnp.concatenate([sums[size * b : size * (b + 1)] for b in part], axis=0)
        for part in (order[:half], order[half:])
    )
    hand_out(bit_ref[0] == 1, low, high, term, send_ref, keep_ref, term_ref)


def middle(outs, w_proj, dz, gain, bit, order):
    tokens, width = dz.shape
    vmem = pl.BlockSpec(memory_space=pltpu.VMEM)
    half = width // 2
    return pl.pallas_call(
        lambda *refs: middle_kernel(order, *refs),
        in_specs=[pl.BlockSpec(memory_space=pltpu.SMEM)] + [vmem] * (len(outs) + 3),
        out_specs=[vmem] * 4,
        out_shape=[
            shape(tokens, width)(BF),
            shape(GAIN_ROWS + half, width)(BF),
            shape(half, width)(F32),
            shape(1, width)(F32),
        ],
        scratch_shapes=[pltpu.VMEM((width, width), F32)],
        compiler_params=params(),
        cost_estimate=pl.CostEstimate(
            flops=8_000_000_000, bytes_accessed=16_000_000, transcendentals=0
        ),
        name="middle",
    )(bit, *outs, w_proj, dz, gain[None])


def add_kernel(bit_ref, got_ref, keep_ref, gain_ref, send_out, keep_out, gain_out):
    half = keep_ref.shape[0] // 2
    total = keep_ref[...] + got_ref[GAIN_ROWS:].astype(F32)
    gain = gain_ref[...] + (got_ref[0:1].astype(F32) + got_ref[1:2].astype(F32))
    hand_out(bit_ref[0] == 1, total[:half], total[half:], gain, send_out, keep_out, gain_out)


def add_step(got, keep, gain, bit):
    rows, width = keep.shape
    vmem = pl.BlockSpec(memory_space=pltpu.VMEM)
    return pl.pallas_call(
        add_kernel,
        in_specs=[pl.BlockSpec(memory_space=pltpu.SMEM)] + [vmem] * 3,
        out_specs=[vmem] * 3,
        out_shape=[
            shape(GAIN_ROWS + rows // 2, width)(BF),
            shape(rows // 2, width)(F32),
            shape(1, width)(F32),
        ],
        compiler_params=params(),
        cost_estimate=pl.CostEstimate(
            flops=rows * width, bytes_accessed=rows * width * 10, transcendentals=0
        ),
        name="add_step",
    )(bit, got, keep, gain)


def last_kernel(norm, got_ref, keep_ref, gain_ref, sum_out, gain_out):
    sum_out[...] = (keep_ref[...] + got_ref[GAIN_ROWS:].astype(F32)) * norm
    gain = gain_ref[...] + (got_ref[0:1].astype(F32) + got_ref[1:2].astype(F32))
    gain_out[...] = gain * norm


def last_step(got, keep, gain, norm):
    vmem = pl.BlockSpec(memory_space=pltpu.VMEM)
    return pl.pallas_call(
        lambda *refs: last_kernel(norm, *refs),
        in_specs=[vmem] * 3,
        out_specs=[vmem] * 2,
        out_shape=[shape(*keep.shape)(F32), shape(*gain.shape)(F32)],
        compiler_params=params(),
        name="last_step",
    )(got, keep, gain)


def back_kernel(core_ref, *refs):
    parts, mine_ref, other_ref, out_ref = refs[:-3], refs[-3], refs[-2], refs[-1]
    left = jnp.concatenate([ref[...] for ref in parts], axis=1)
    first = core_ref[0] == 0
    rows = 64
    blocks = []
    for z in range(mine_ref.shape[0] // rows):
        mine, other = mine_ref[rows * z : rows * (z + 1)], other_ref[rows * z : rows * (z + 1)]
        blocks += [jnp.where(first, mine, other), jnp.where(first, other, mine)]
    for n in range(len(blocks) // 4):
        right = jnp.concatenate(blocks[4 * n : 4 * n + 4], axis=0)
        out_ref[:, 256 * n : 256 * (n + 1)] = lax.dot_general(
            left, right, NT, preferred_element_type=F32
        ).astype(BF)


def back_product(parts, mine, other, core):
    vmem = pl.BlockSpec(memory_space=pltpu.VMEM)
    return pl.pallas_call(
        back_kernel,
        in_specs=[pl.BlockSpec(memory_space=pltpu.SMEM)] + [vmem] * (len(parts) + 2),
        out_specs=vmem,
        out_shape=shape(parts[0].shape[0], 2 * mine.shape[0])(BF),
        compiler_params=params(),
        cost_estimate=pl.CostEstimate(
            flops=5_000_000_000, bytes_accessed=11_000_000, transcendentals=0
        ),
        name="back_product",
    )(core, *parts, mine, other)


def block_order(row_count, col_count):
    count = row_count * col_count
    bits = [s for s in STEPS if s[0] != "dp"]
    order = []
    for place in range(count):
        row = col = 0
        for n, (axis, bit) in enumerate(bits):
            if place >> (len(bits) - 1 - n) & 1:
                row, col = (row | bit, col) if axis == "row" else (row, col | bit)
        order.append(row * col_count + col)
    return order


def exchange(value, axis, bit):
    pairs = [(i, i ^ bit) for i in range(lax.axis_size(axis))]
    return lax.ppermute(value, axis, pairs)


def shift(value, rows, cols, step):
    r, c = lax.axis_size("row"), lax.axis_size("col")
    if rows and cols:
        pairs = [
            (i * c + j, (i + step) % r * c + (j + step) % c) for i in range(r) for j in range(c)
        ]
        return lax.ppermute(value, ("row", "col"), pairs)
    name, count = ("row", r) if rows else ("col", c)
    return lax.ppermute(value, name, [(i, (i + step) % count) for i in range(count)])


def quadrant(values, low_row, low_col):
    half = values.shape[0] // 2
    rows = slice(0, half) if low_row else slice(half, None)
    cols = slice(0, half) if low_col else slice(half, None)
    return values[rows, cols]


def per_device(qkv, grad_out, w_qkv, w_proj, norm_gain, region):
    side, width = grad_out.shape[1], grad_out.shape[3]
    half = side // 2
    tokens = side * side
    grad = grad_out[0]
    flat = (half * half, width)
    square = (half, half, width)

    def send(value, rows, cols, step):
        return shift(value.reshape(flat), rows, cols, step).reshape(square)

    core = lax.axis_index("col") % 2
    rows = w_qkv.shape[0] // 2
    mine = lax.all_gather(
        lax.dynamic_slice_in_dim(w_qkv, core * rows, rows, 0), "dp", axis=0, tiled=True
    )
    from_row = send(quadrant(grad, True, False), True, False, -1)
    from_col = send(quadrant(grad, False, True), False, True, -1)
    from_both = send(quadrant(grad, True, True), True, True, -1)

    ids = region.reshape(tokens, 1)
    lane = lax.broadcasted_iota(jnp.int32, (tokens, 128), 1)
    hot = (ids == lane).astype(BF)
    mask = jnp.where((lane < 4) & (ids != lane), -1e30, 0.0).astype(BF)
    qkv_t = qkv.reshape(tokens, 3 * width)
    chunks = 4
    per = width // 128 // chunks
    fwd = [forward(qkv_t, hot, mask, per * n, per) for n in range(chunks)]

    dz = jnp.concatenate(
        [
            jnp.concatenate([quadrant(grad, False, False), from_col], axis=1),
            jnp.concatenate([from_row, from_both], axis=1),
        ],
        axis=0,
    ).reshape(tokens, width)

    def bit_of(axis, bit):
        return (lax.axis_index(axis) // bit % 2).astype(jnp.int32).reshape(1)

    r, c, d = lax.axis_size("row"), lax.axis_size("col"), lax.axis_size("dp")
    dattn, wire, keep, gain = middle(
        [f[1] for f in fwd], w_proj, dz, norm_gain, bit_of(*STEPS[0]), block_order(r, c)
    )
    other = exchange(mine, "col", 1)
    norm = (tokens * r * c * d) ** (-0.5)
    for n, step in enumerate(STEPS):
        got = exchange(wire, *step)
        if n + 1 < len(STEPS):
            wire, keep, gain = add_step(got, keep, gain, bit_of(*STEPS[n + 1]))
        else:
            grad_proj, grad_gain = last_step(got, keep, gain, norm)

    bwd = [
        backward(f[0], qkv_t, dattn, f[1], f[2], per * n, per) for n, f in enumerate(fwd)
    ]
    parts = [b[i] for i in range(3) for b in bwd]
    back = back_product(parts, mine, other, core.astype(jnp.int32).reshape(1))
    back = back.reshape(side, side, width)
    to_row = send(quadrant(back, False, True), True, False, 1)
    to_col = send(quadrant(back, True, False), False, True, 1)
    to_both = send(quadrant(back, False, False), True, True, 1)
    moved = jnp.concatenate(
        [
            jnp.concatenate([to_both, to_row], axis=1),
            jnp.concatenate([to_col, quadrant(back, True, True)], axis=1),
        ],
        axis=0,
    )
    grad_in = (grad.astype(F32) + moved.astype(F32)).astype(BF)[None]
    return (grad_in, grad_proj, grad_gain[0])


def solution(mesh):
    return jax.shard_map(
        per_device,
        mesh=mesh,
        in_specs=(
            P("dp", "row", "col", None),
            P("dp", "row", "col", None),
            P("dp", None),
            P(),
            P(),
            P("row", "col"),
        ),
        out_specs=(P("dp", "row", "col", None), P(("row", "col", "dp"), None), P()),
        check_vma=False,
    )
```

```python
import math

import jax
import jax.numpy as jnp
from jax import lax
from jax.experimental import pallas as pl
from jax.experimental.pallas import tpu as pltpu
from jax.sharding import PartitionSpec as P

HEADS = 32
GROUP = 4
BF = jnp.bfloat16
F32 = jnp.float32
NT = (((1,), (1,)), ((), ()))
TN = (((0,), (0,)), ((), ()))
LIMIT = 56 * 2**20
GAIN_ROWS = 8
RADIX = 4
REGIONS = 4


def params():
    return pltpu.CompilerParams(vmem_limit_bytes=LIMIT)


def shape(*dims):
    return lambda kind: jax.ShapeDtypeStruct(dims, kind)


def split3(value):
    high = value.astype(BF)
    rest = value - high.astype(F32)
    mid = rest.astype(BF)
    return high, mid, (rest - mid.astype(F32)).astype(BF)


def forward_kernel(q_ref, k_ref, v_ref, hot_ref, p_ref, o_ref, inv_ref):
    tokens, lanes = q_ref.shape
    size = lanes // GROUP
    factor = size ** (-0.5) * math.log2(math.e)
    queries, keys, values, hot = q_ref[...], k_ref[...], v_ref[...], hot_ref[...]
    lane = lax.broadcasted_iota(jnp.int32, (tokens, lanes), 1)
    head = lane // size
    mask = jnp.where(lane % size < REGIONS, (hot.astype(F32) - 1.0) * 1e30, 0.0).astype(BF)

    def scores_of(h):
        left, right = jnp.where(head == h, queries, hot), jnp.where(head == h, keys, mask)
        return lax.dot_general(left, right, NT, preferred_element_type=F32)

    def attend(h, expo):
        summed = jnp.where(head == h, values, jnp.ones_like(values))
        both = jnp.dot(expo, summed, preferred_element_type=F32)
        inv = 1.0 / pltpu.roll(both, size, axis=1)
        return both * inv, inv

    scores = scores_of(0)
    last, out, inverse = None, None, None
    for h in range(GROUP + 1):
        ahead = scores_of(h + 1) if h + 1 < GROUP else None
        if last is not None:
            attn, inv = attend(h - 1, last)
            out = attn if out is None else jnp.where(head == h - 1, attn, out)
            inverse = inv if inverse is None else jnp.where(head == h - 1, inv, inverse)
        if h < GROUP:
            top = jnp.max(scores, axis=1, keepdims=True)
            last = jnp.exp2((scores - top) * factor).astype(BF)
            p_ref[h] = last
        scores = ahead
    o_ref[...] = out
    inv_ref[...] = inverse


def backward_kernel(p_ref, q_ref, k_ref, v_ref, do_ref, o_ref, inv_ref, dq_ref, dk_ref, dv_ref):
    tokens, lanes = q_ref.shape
    size = lanes // GROUP
    scale = size ** (-0.5)
    keys, values, dout, inv = k_ref[...], v_ref[...], do_ref[...], inv_ref[...]
    lane = lax.broadcasted_iota(jnp.int32, (tokens, lanes), 1)
    head = lane // size
    dout_f = dout.astype(F32)
    row_i = lax.broadcasted_iota(jnp.int32, (lanes, lanes), 0) // size
    col_i = lax.broadcasted_iota(jnp.int32, (lanes, lanes), 1)
    pick = jnp.where((col_i // size == (row_i + 1) % GROUP) & (col_i % size < 3), 1.0, 0.0).astype(BF)
    parts = jnp.concatenate(split3(dout_f * o_ref[...]), axis=1)
    delta = jnp.dot(parts, jnp.concatenate([pick] * 3, axis=0), preferred_element_type=F32)
    d_high = delta.astype(BF).astype(F32)
    d_rest = delta - d_high
    d_mid = d_rest.astype(BF).astype(F32)
    which = lane % size
    columns = jnp.where(
        which == 0, d_high, jnp.where(which == 1, d_mid, jnp.where(which == 2, d_rest - d_mid, 0.0))
    ).astype(BF)
    dout_t = (dout_f * inv).T.astype(BF)
    query_t = (q_ref[...].astype(F32) * (inv * scale)).T.astype(BF)

    def dprobs_of(h):
        minus = jnp.where((head == (h + 1) % GROUP) & (which < 3), -1.0, 0.0).astype(BF)
        left, right = jnp.where(head == h, dout, columns), jnp.where(head == h, values, minus)
        return lax.dot_general(left, right, NT, preferred_element_type=F32)

    dprobs = dprobs_of(0)
    dq, dks, dvs = None, [], []
    for h in range(GROUP):
        ahead = dprobs_of(h + 1) if h + 1 < GROUP else None
        probs = p_ref[h]
        dscores = (probs.astype(F32) * dprobs).astype(BF)
        part = jnp.dot(dscores, keys, preferred_element_type=F32)
        dq = part if dq is None else jnp.where(head == h, part, dq)
        rows = slice(size * h, size * (h + 1))
        dks.append(jnp.dot(query_t[rows], dscores, preferred_element_type=F32))
        dvs.append(jnp.dot(dout_t[rows], probs, preferred_element_type=F32))
        dprobs = ahead
    dq_ref[...] = (dq * (inv * scale)).astype(BF)
    dk_ref[...] = jnp.concatenate(dks, axis=0).T.astype(BF)
    dv_ref[...] = jnp.concatenate(dvs, axis=0).T.astype(BF)


def column_block(tokens, offset):
    return pl.BlockSpec((tokens, 128), lambda g: (0, g + offset))


def forward(qkv, hot, first, count):
    tokens = qkv.shape[0]
    per = qkv.shape[1] // 3 // 128
    whole = pl.BlockSpec((tokens, 128), lambda g: (0, 0))
    out = shape(tokens, count * 128)(F32)
    return pl.pallas_call(
        forward_kernel,
        grid=(count,),
        in_specs=[column_block(tokens, first + per * i) for i in range(3)] + [whole],
        out_specs=[pl.BlockSpec((GROUP, tokens, tokens), lambda g: (g, 0, 0))]
        + [column_block(tokens, 0)] * 2,
        out_shape=[shape(count * GROUP, tokens, tokens)(BF), out, out],
        compiler_params=params(),
        cost_estimate=pl.CostEstimate(
            flops=count * 3_200_000_000, bytes_accessed=count * 4_000_000, transcendentals=0
        ),
        name="attn_forward",
    )(qkv, qkv, qkv, hot)


def backward(probs, qkv, dattn, out, inverse, first, count):
    tokens = qkv.shape[0]
    per = qkv.shape[1] // 3 // 128
    return pl.pallas_call(
        backward_kernel,
        grid=(count,),
        in_specs=[pl.BlockSpec((GROUP, tokens, tokens), lambda g: (g + first, 0, 0))]
        + [column_block(tokens, first + per * i) for i in range(3)]
        + [column_block(tokens, first)] * 3,
        out_specs=[column_block(tokens, 0)] * 3,
        out_shape=[shape(tokens, count * 128)(BF)] * 3,
        compiler_params=params(),
        cost_estimate=pl.CostEstimate(
            flops=count * 3_600_000_000, bytes_accessed=count * 4_000_000, transcendentals=0
        ),
        name="attn_backward",
    )(probs, qkv, qkv, qkv, dattn, out, inverse)


def pack_gain(high, low):
    rows = lax.broadcasted_iota(jnp.int32, (GAIN_ROWS, high.shape[1]), 0)
    return jnp.where(rows == 0, high, jnp.where(rows == 1, low, 0.0)).astype(BF)


def middle_kernel(order, bit_ref, *refs):
    outs, (w_ref, dz_ref, gain_ref, do_ref, send_ref, keep_ref, term_ref, sums) = refs[:-8], refs[-8:]
    attn = jnp.concatenate([ref[...].astype(BF) for ref in outs], axis=1)
    weights = w_ref[...]
    proj = jnp.dot(attn, weights, preferred_element_type=F32)
    centred = proj - jnp.mean(proj, axis=1, keepdims=True)
    rstd = lax.rsqrt(jnp.mean(centred * centred, axis=1, keepdims=True) + 1e-05)
    normed = centred * rstd
    dz = dz_ref[...].astype(F32)
    term = jnp.sum(dz * normed, axis=0, keepdims=True)
    scaled = dz * gain_ref[...]
    mean = jnp.mean(scaled, axis=1, keepdims=True)
    dot = jnp.mean(scaled * normed, axis=1, keepdims=True)
    dproj = (rstd * (scaled - mean - normed * dot)).astype(BF)
    do_ref[...] = lax.dot_general(dproj, weights, NT, preferred_element_type=F32).astype(BF)
    sums[...] = lax.dot_general(attn, dproj, TN, preferred_element_type=F32)
    half = len(order) // 2
    size = sums.shape[0] // len(order)
    low, high = (
        jnp.concatenate([sums[size * b : size * (b + 1)] for b in part], axis=0)
        for part in (order[:half], order[half:])
    )
    second = bit_ref[0] == 1
    term_high = term.astype(BF).astype(F32)
    term_low = (term - term_high).astype(BF).astype(F32)
    send_ref[0:GAIN_ROWS] = pack_gain(term_high, term_low)
    send_ref[GAIN_ROWS:] = jnp.where(second, low, high).astype(BF)
    keep_ref[...] = jnp.where(second, high, low)
    term_ref[...] = term_high + term_low


def middle(outs, w_proj, dz, gain, bit, order):
    tokens, width = dz.shape
    vmem = pl.BlockSpec(memory_space=pltpu.VMEM)
    half = width // 2
    return pl.pallas_call(
        lambda *refs: middle_kernel(order, *refs),
        in_specs=[pl.BlockSpec(memory_space=pltpu.SMEM)] + [vmem] * (len(outs) + 3),
        out_specs=[vmem] * 4,
        out_shape=[
            shape(tokens, width)(BF),
            shape(GAIN_ROWS + half, width)(BF),
            shape(half, width)(F32),
            shape(1, width)(F32),
        ],
        scratch_shapes=[pltpu.VMEM((width, width), F32)],
        compiler_params=params(),
        cost_estimate=pl.CostEstimate(
            flops=8_000_000_000, bytes_accessed=16_000_000, transcendentals=0
        ),
        name="middle",
    )(bit, *outs, w_proj, dz, gain[None])


def back_kernel(core_ref, *refs):
    parts, (mine_ref, other_ref), outs = refs[:6], refs[6:8], refs[8:]
    first = core_ref[0] == 0
    left = jnp.concatenate([ref[...] for ref in parts], axis=1)
    rows = 64
    blocks = []
    for z in range(mine_ref.shape[0] // rows):
        mine, other = mine_ref[rows * z : rows * (z + 1)], other_ref[rows * z : rows * (z + 1)]
        blocks += [jnp.where(first, mine, other), jnp.where(first, other, mine)]
    total = lax.dot_general(left, jnp.concatenate(blocks, axis=0), NT, preferred_element_type=F32)
    side = math.isqrt(total.shape[0])
    half = side // 2
    for n, ref in enumerate(outs):
        start = side * half * (n // 2) + half * (n % 2)
        ref[...] = jnp.concatenate(
            [total[start + side * i : start + side * i + half] for i in range(half)], axis=0
        ).astype(BF)


def back_product(parts, mine, other, core, which):
    tokens = parts[0].shape[0]
    rows, inner = mine.shape
    steps = 2
    wide = 2 * rows // (2 * steps)
    side = pl.BlockSpec((rows // (2 * steps), inner), lambda g: (g + which * steps, 0))
    out = pl.BlockSpec((tokens // 4, wide), lambda g: (0, g))
    return pl.pallas_call(
        back_kernel,
        grid=(steps,),
        in_specs=[pl.BlockSpec(memory_space=pltpu.SMEM)]
        + [pl.BlockSpec(part.shape, lambda g: (0, 0)) for part in parts]
        + [side] * 2,
        out_specs=[out] * 4,
        out_shape=[shape(tokens // 4, wide * steps)(BF)] * 4,
        compiler_params=params(),
        cost_estimate=pl.CostEstimate(
            flops=2_500_000_000, bytes_accessed=8_000_000, transcendentals=0
        ),
        name="back_product",
    )(core, *parts, mine, other)


def position(row, col):
    return row // 2, row % 2 * 2 + col // 2, col % 2


def place(x, y, core):
    return x * 2 + y // 2, y % 2 * 2 + core


def block_order(row_count, col_count):
    order = []
    for core in range(2):
        for first in range(RADIX):
            for second in range(RADIX):
                x, y = (first, second) if core == 0 else (second, first)
                row, col = place(x, y, core)
                order.append(row * col_count + col)
    return order


def plane_pairs(rows, cols, turn, step):
    pairs = []
    for r in range(rows):
        for c in range(cols):
            x, y, core = position(r, c)
            if core == turn:
                x = (x + step) % RADIX
            else:
                y = (y + step) % RADIX
            to_r, to_c = place(x, y, core)
            pairs.append((r * cols + c, to_r * cols + to_c))
    return pairs


def round_pieces(total, gain, index, count):
    rows = total.shape[0] // count
    high = lax.reduce_precision(gain, 8, 7)
    low = lax.reduce_precision(gain - high, 8, 7)
    packed = pack_gain(high, low)
    pieces = [
        jnp.concatenate(
            [
                packed,
                lax.dynamic_slice_in_dim(total, (index + n) % count * rows, rows, 0).astype(BF),
            ],
            axis=0,
        )
        for n in range(1, count)
    ]
    return pieces, lax.dynamic_slice_in_dim(total, index * rows, rows, 0), high + low


def round_sums(got, own, gain, index):
    count = len(got) + 1
    gains = [gain]
    for value in got:
        own = own + value[GAIN_ROWS:].astype(F32)
        gains.append(value[0:1].astype(F32) + value[1:2].astype(F32))
    turned = jnp.concatenate(gains[::-1] * 2, axis=0)
    ordered = lax.dynamic_slice_in_dim(turned, count - 1 - index, count, 0)
    gain = ordered[0:1]
    for n in range(1, count):
        gain = gain + ordered[n : n + 1]
    return own, gain


def shift(value, rows, cols, step):
    r, c = lax.axis_size("row"), lax.axis_size("col")
    if rows and cols:
        pairs = [
            (i * c + j, (i + step) % r * c + (j + step) % c) for i in range(r) for j in range(c)
        ]
        return lax.ppermute(value, ("row", "col"), pairs)
    name, count = ("row", r) if rows else ("col", c)
    return lax.ppermute(value, name, [(i, (i + step) % count) for i in range(count)])


def quadrant(values, low_row, low_col):
    half = values.shape[0] // 2
    rows = slice(0, half) if low_row else slice(half, None)
    cols = slice(0, half) if low_col else slice(half, None)
    return values[rows, cols]


def per_device(qkv, grad_out, w_qkv, w_proj, norm_gain, region):
    side, width = grad_out.shape[1], grad_out.shape[3]
    half = side // 2
    tokens = side * side
    grad = grad_out[0]
    flat = (half * half, width)
    square = (half, half, width)

    def send(value, rows, cols, step):
        return shift(value.reshape(flat), rows, cols, step).reshape(square)

    core = lax.axis_index("col") % 2
    rows = w_qkv.shape[0] // 2
    mine_w = lax.dynamic_slice_in_dim(w_qkv, core * rows, rows, 0)
    mine = lax.all_gather(mine_w, "dp", axis=0, tiled=True)
    from_row = send(quadrant(grad, True, False), True, False, -1)
    from_col = send(quadrant(grad, False, True), False, True, -1)
    from_both = send(quadrant(grad, True, True), True, True, -1)

    ids = region.reshape(tokens, 1)
    lane = lax.broadcasted_iota(jnp.int32, (tokens, 128), 1)
    hot = (ids == lane % (width // HEADS)).astype(BF)
    qkv_t = qkv.reshape(tokens, 3 * width)
    groups = width // 128
    qkv_t, mine_w = lax.optimization_barrier((qkv_t, mine_w))
    probs, out, inverse = forward(qkv_t, hot, 0, groups)

    dz = jnp.concatenate(
        [
            jnp.concatenate([quadrant(grad, False, False), from_col], axis=1),
            jnp.concatenate([from_row, from_both], axis=1),
        ],
        axis=0,
    ).reshape(tokens, width)

    r, c, d = lax.axis_size("row"), lax.axis_size("col"), lax.axis_size("dp")
    row, col, dp = lax.axis_index("row"), lax.axis_index("col"), lax.axis_index("dp")
    bit = core.astype(jnp.int32).reshape(1)
    dattn, wire, keep, gain = middle([out], w_proj, dz, norm_gain, bit, block_order(r, c))
    other = lax.ppermute(mine, "col", [(i, i ^ 1) for i in range(c)])
    norm = (tokens * r * c * d) ** (-0.5)
    got = lax.ppermute(wire, "col", [(i, i ^ 1) for i in range(c)])
    x, y, _ = position(row, col)

    def plane_round(pieces, turn):
        return [
            lax.ppermute(piece, ("row", "col"), plane_pairs(r, c, turn, n + 1))
            for n, piece in enumerate(pieces)
        ]

    half_groups = groups // 2
    early = backward(probs, qkv_t, dattn, out, inverse, 0, half_groups)
    early, got = lax.optimization_barrier((early, got))
    sums = keep + got[GAIN_ROWS:].astype(F32)
    gain = gain + (got[0:1].astype(F32) + got[1:2].astype(F32))
    index = jnp.where(core == 0, x, y)
    pieces, own, gain = round_pieces(sums, gain, index, RADIX)
    dattn, pieces = lax.optimization_barrier((dattn, pieces))
    got = plane_round(pieces, 0)

    late = backward(probs, qkv_t, dattn, out, inverse, half_groups, half_groups)
    late, got = lax.optimization_barrier((late, got))
    sums, gain = round_sums(got, own, gain, index)
    index = jnp.where(core == 0, y, x)
    pieces, own, gain = round_pieces(sums, gain, index, RADIX)
    late, pieces = lax.optimization_barrier((late, pieces))
    got = plane_round(pieces, 1)

    parts = [part for pair in zip(early, late) for part in pair]
    moved = []
    for n in range(2):
        quarters = back_product(parts, mine, other, bit, n)
        if n == 1:
            quarters, got = lax.optimization_barrier((quarters, got))
        moved.append(
            [quarters[0]] + [shift(quarters[i], i // 2 == 1, i % 2 == 1, 1) for i in (1, 2, 3)]
        )

    sums, gain = round_sums(got, own, gain, index)
    pieces, own, gain = round_pieces(sums, gain, dp, d)
    got = [
        lax.ppermute(piece, "dp", [(i, (i + n + 1) % d) for i in range(d)])
        for n, piece in enumerate(pieces)
    ]
    sums, gain = round_sums(got, own, gain, dp)
    grad_proj, grad_gain = sums * norm, gain * norm

    local, to_col, to_row, to_both = (
        jnp.concatenate(pair, axis=1).reshape(square) for pair in zip(*moved)
    )
    moved = jnp.concatenate(
        [
            jnp.concatenate([to_both, to_row], axis=1),
            jnp.concatenate([to_col, local], axis=1),
        ],
        axis=0,
    )
    grad_in = (grad.astype(F32) + moved.astype(F32)).astype(BF)[None]
    return (grad_in, grad_proj, grad_gain[0])


def solution(mesh):
    return jax.shard_map(
        per_device,
        mesh=mesh,
        in_specs=(
            P("dp", "row", "col", None),
            P("dp", "row", "col", None),
            P("dp", None),
            P(),
            P(),
            P("row", "col"),
        ),
        out_specs=(P("dp", "row", "col", None), P(("row", "col", "dp"), None), P()),
        check_vma=False,
    )
```

```python
import math

import jax
import jax.numpy as jnp
from jax import lax
from jax.experimental import pallas as pl
from jax.experimental.pallas import tpu as pltpu
from jax.sharding import PartitionSpec as P

HEADS = 32
GROUP = 4
BF = jnp.bfloat16
F32 = jnp.float32
NT = (((1,), (1,)), ((), ()))
TN = (((0,), (0,)), ((), ()))
LIMIT = 56 * 2**20
GAIN_ROWS = 8
RADIX = 4
REGIONS = 4


def params():
    return pltpu.CompilerParams(vmem_limit_bytes=LIMIT)


def shape(*dims):
    return lambda kind: jax.ShapeDtypeStruct(dims, kind)


def split3(value):
    high = value.astype(BF)
    rest = value - high.astype(F32)
    mid = rest.astype(BF)
    return high, mid, (rest - mid.astype(F32)).astype(BF)


def by_head(parts):
    return jnp.concatenate(parts, axis=0)


def zero_unless(chosen, value):
    return jnp.where(chosen, value, jnp.zeros_like(value))


def forward_kernel(q_ref, k_ref, v_ref, hot_ref, p_ref, rest_ref, o_ref, inv_ref):
    tokens, lanes = q_ref.shape
    size = lanes // GROUP
    main = p_ref.shape[2]
    tail = tokens - main
    factor = size ** (-0.5) * math.log2(math.e)
    queries, keys, values, hot = q_ref[...], k_ref[...], v_ref[...], hot_ref[...]
    lane = lax.broadcasted_iota(jnp.int32, (tokens, lanes), 1)
    head = lane // size
    mask = jnp.where(lane % size < REGIONS, (hot.astype(F32) - 1.0) * 1e30, 0.0).astype(BF)
    tail_keys, tail_values, tail_head = keys[main:], values[main:], head[:tail]
    tail_mask = zero_unless(tail_head == 0, mask[main:])
    tail_scores = lax.dot_general(
        jnp.concatenate([queries, hot], axis=1),
        jnp.concatenate(
            [
                by_head([zero_unless(tail_head == h, tail_keys) for h in range(GROUP)]),
                by_head([tail_mask] * GROUP),
            ],
            axis=1,
        ),
        NT,
        preferred_element_type=F32,
    )
    per = lanes // tail
    main_head = head[:main]

    def scores_of(h):
        left = jnp.where(head == h, queries, hot)
        right = jnp.where(main_head == h, keys[:main], mask[:main])
        return lax.dot_general(left, right, NT, preferred_element_type=F32)

    scores = scores_of(0)
    last, sums, tops = None, [], []
    for h in range(GROUP + 1):
        ahead = scores_of(h + 1) if h + 1 < GROUP else None
        if last is not None:
            own = main_head == h - 1
            summed = jnp.where(own, values[:main], jnp.ones_like(values[:main]))
            sums.append(jnp.dot(last, summed, preferred_element_type=F32))
        if h < GROUP:
            tile = tail_scores[:, lanes * (h // per) : lanes * (h // per + 1)]
            top = jnp.where(lane // tail == h % per, tile, -3e38)
            for start in range(0, main, lanes):
                top = jnp.maximum(top, scores[:, start : start + lanes])
            tops.append(jnp.max(top, axis=1, keepdims=True))
            last = jnp.exp2((scores - tops[h]) * factor).astype(BF)
            p_ref[h] = last
        scores = ahead
    rest = []
    for n in range(GROUP // per):
        top = tops[n * per]
        for i in range(1, per):
            top = jnp.where(lane // tail == i, tops[n * per + i], top)
        tile = tail_scores[:, lanes * n : lanes * (n + 1)]
        rest.append(jnp.exp2((tile - top) * factor).astype(BF))
    rest = jnp.concatenate(rest, axis=1)
    rest_ref[...] = rest
    ones = jnp.ones_like(tail_values)
    right = by_head(
        [
            jnp.concatenate(
                [zero_unless(tail_head == h, tail_values), zero_unless(tail_head == h, ones)], axis=1
            )
            for h in range(GROUP)
        ]
    )
    both = jnp.dot(rest, right, preferred_element_type=F32)
    out, total = None, None
    for h, part in enumerate(sums):
        turned = pltpu.roll(part, size, axis=1)
        out = part if out is None else jnp.where(head == h, part, out)
        total = turned if total is None else jnp.where(head == h, turned, total)
    inverse = 1.0 / (total + both[:, lanes:])
    o_ref[...] = (out + both[:, :lanes]) * inverse
    inv_ref[...] = inverse


def backward_kernel(
    p_ref, rest_ref, q_ref, k_ref, v_ref, do_ref, o_ref, inv_ref, dq_ref, dk_ref, dv_ref
):
    tokens, lanes = q_ref.shape
    size = lanes // GROUP
    main = p_ref.shape[2]
    tail = tokens - main
    scale = size ** (-0.5)
    keys, values, dout, inv = k_ref[...], v_ref[...], do_ref[...], inv_ref[...]
    lane = lax.broadcasted_iota(jnp.int32, (tokens, lanes), 1)
    head, which = lane // size, lane % size
    dout_f = dout.astype(F32)
    row_i = lax.broadcasted_iota(jnp.int32, (lanes, lanes), 0) // size
    col_i = lax.broadcasted_iota(jnp.int32, (lanes, lanes), 1)
    pick = jnp.where((col_i // size == (row_i + 1) % GROUP) & (col_i % size < 3), 1.0, 0.0).astype(BF)
    parts = jnp.concatenate(split3(dout_f * o_ref[...]), axis=1)
    delta = jnp.dot(parts, jnp.concatenate([pick] * 3, axis=0), preferred_element_type=F32)
    d_high = delta.astype(BF).astype(F32)
    d_rest = delta - d_high
    d_mid = d_rest.astype(BF).astype(F32)
    columns = jnp.where(
        which == 0, d_high, jnp.where(which == 1, d_mid, jnp.where(which == 2, d_rest - d_mid, 0.0))
    ).astype(BF)
    dout_t = (dout_f * inv).T.astype(BF)
    query_t = (q_ref[...].astype(F32) * (inv * scale)).T.astype(BF)
    tail_head, main_head = head[:tail], head[:main]

    def minus(h, count):
        chosen = (head[:count] == (h + 1) % GROUP) & (which[:count] < 3)
        return jnp.where(chosen, -1.0, 0.0).astype(BF)

    rest = rest_ref[...]
    right = by_head(
        [
            jnp.concatenate([zero_unless(tail_head == h, values[main:]), minus(h, tail)], axis=1)
            for h in range(GROUP)
        ]
    )
    dprobs = lax.dot_general(
        jnp.concatenate([dout, columns], axis=1), right, NT, preferred_element_type=F32
    )
    dscores_rest = (rest.astype(F32) * dprobs).astype(BF)

    def dprobs_of(h):
        left = jnp.where(head == h, dout, columns)
        right = jnp.where(main_head == h, values[:main], minus(h, main))
        return lax.dot_general(left, right, NT, preferred_element_type=F32)

    dprobs = dprobs_of(0)
    dq, dks, dvs = None, [], []
    for h in range(GROUP):
        ahead = dprobs_of(h + 1) if h + 1 < GROUP else None
        probs = p_ref[h]
        dscores = (probs.astype(F32) * dprobs).astype(BF)
        part = jnp.dot(dscores, keys[:main], preferred_element_type=F32)
        dq = part if dq is None else jnp.where(head == h, part, dq)
        rows = slice(size * h, size * (h + 1))
        dks.append(jnp.dot(query_t[rows], dscores, preferred_element_type=F32))
        dvs.append(jnp.dot(dout_t[rows], probs, preferred_element_type=F32))
        dprobs = ahead
    right = by_head([zero_unless(tail_head == h, keys[main:]) for h in range(GROUP)])
    dq = dq + jnp.dot(dscores_rest, right, preferred_element_type=F32)
    dq_ref[...] = (dq * (inv * scale)).astype(BF)
    for ref, whole, left, right in (
        (dk_ref, dks, query_t, dscores_rest),
        (dv_ref, dvs, dout_t, rest),
    ):
        ref[0:main] = jnp.concatenate(whole, axis=0).T.astype(BF)
        turned = jnp.dot(left, right, preferred_element_type=F32).T
        last = turned[0:tail]
        for h in range(1, GROUP):
            last = jnp.where(tail_head == h, turned[tail * h : tail * (h + 1)], last)
        ref[main:] = last.astype(BF)


def column_block(tokens, offset):
    return pl.BlockSpec((tokens, 128), lambda g: (0, g + offset))


def forward(qkv, hot):
    tokens = qkv.shape[0]
    per = qkv.shape[1] // 3 // 128
    main = tokens // 256 * 256
    rest = (tokens - main) * GROUP
    out = shape(tokens, per * 128)(F32)
    return pl.pallas_call(
        forward_kernel,
        grid=(per,),
        in_specs=[column_block(tokens, per * i) for i in range(3)]
        + [pl.BlockSpec((tokens, 128), lambda g: (0, 0))],
        out_specs=[
            pl.BlockSpec((GROUP, tokens, main), lambda g: (g, 0, 0)),
            pl.BlockSpec((tokens, rest), lambda g: (0, g)),
        ]
        + [column_block(tokens, 0)] * 2,
        out_shape=[
            shape(per * GROUP, tokens, main)(BF),
            shape(tokens, per * rest)(BF),
            out,
            out,
        ],
        compiler_params=params(),
        cost_estimate=pl.CostEstimate(
            flops=per * 3_200_000_000, bytes_accessed=per * 4_000_000, transcendentals=0
        ),
        name="attn_forward",
    )(qkv, qkv, qkv, hot)


def backward(probs, rest, qkv, dattn, out, inverse, first, count):
    tokens = qkv.shape[0]
    per = qkv.shape[1] // 3 // 128
    return pl.pallas_call(
        backward_kernel,
        grid=(count,),
        in_specs=[
            pl.BlockSpec((GROUP, *probs.shape[1:]), lambda g: (g + first, 0, 0)),
            pl.BlockSpec((tokens, rest.shape[1] // per), lambda g: (0, g + first)),
        ]
        + [column_block(tokens, first + per * i) for i in range(3)]
        + [column_block(tokens, first)] * 3,
        out_specs=[column_block(tokens, 0)] * 3,
        out_shape=[shape(tokens, count * 128)(BF)] * 3,
        compiler_params=params(),
        cost_estimate=pl.CostEstimate(
            flops=count * 3_600_000_000, bytes_accessed=count * 4_000_000, transcendentals=0
        ),
        name="attn_backward",
    )(probs, rest, qkv, qkv, qkv, dattn, out, inverse)


def pack_gain(high, low):
    rows = lax.broadcasted_iota(jnp.int32, (GAIN_ROWS, high.shape[1]), 0)
    return jnp.where(rows == 0, high, jnp.where(rows == 1, low, 0.0)).astype(BF)


def middle_kernel(order, bit_ref, *refs):
    outs, (w_ref, dz_ref, gain_ref, do_ref, send_ref, keep_ref, term_ref, sums) = refs[:-8], refs[-8:]
    attn = jnp.concatenate([ref[...].astype(BF) for ref in outs], axis=1)
    weights = w_ref[...]
    proj = jnp.dot(attn, weights, preferred_element_type=F32)
    centred = proj - jnp.mean(proj, axis=1, keepdims=True)
    rstd = lax.rsqrt(jnp.mean(centred * centred, axis=1, keepdims=True) + 1e-05)
    normed = centred * rstd
    dz = dz_ref[...].astype(F32)
    term = jnp.sum(dz * normed, axis=0, keepdims=True)
    scaled = dz * gain_ref[...]
    mean = jnp.mean(scaled, axis=1, keepdims=True)
    dot = jnp.mean(scaled * normed, axis=1, keepdims=True)
    dproj = (rstd * (scaled - mean - normed * dot)).astype(BF)
    do_ref[...] = lax.dot_general(dproj, weights, NT, preferred_element_type=F32).astype(BF)
    sums[...] = lax.dot_general(attn, dproj, TN, preferred_element_type=F32)
    half = len(order) // 2
    size = sums.shape[0] // len(order)
    low, high = (
        jnp.concatenate([sums[size * b : size * (b + 1)] for b in part], axis=0)
        for part in (order[:half], order[half:])
    )
    second = bit_ref[0] == 1
    term_high = term.astype(BF).astype(F32)
    term_low = (term - term_high).astype(BF).astype(F32)
    send_ref[0:GAIN_ROWS] = pack_gain(term_high, term_low)
    send_ref[GAIN_ROWS:] = jnp.where(second, low, high).astype(BF)
    keep_ref[...] = jnp.where(second, high, low)
    term_ref[...] = term_high + term_low


def middle(outs, w_proj, dz, gain, bit, order):
    tokens, width = dz.shape
    vmem = pl.BlockSpec(memory_space=pltpu.VMEM)
    half = width // 2
    return pl.pallas_call(
        lambda *refs: middle_kernel(order, *refs),
        in_specs=[pl.BlockSpec(memory_space=pltpu.SMEM)] + [vmem] * (len(outs) + 3),
        out_specs=[vmem] * 4,
        out_shape=[
            shape(tokens, width)(BF),
            shape(GAIN_ROWS + half, width)(BF),
            shape(half, width)(F32),
            shape(1, width)(F32),
        ],
        scratch_shapes=[pltpu.VMEM((width, width), F32)],
        compiler_params=params(),
        cost_estimate=pl.CostEstimate(
            flops=8_000_000_000, bytes_accessed=16_000_000, transcendentals=0
        ),
        name="middle",
    )(bit, *outs, w_proj, dz, gain[None])


def back_kernel(core_ref, *refs):
    parts, (mine_ref, other_ref), outs = refs[:-6], refs[-6:-4], refs[-4:]
    first = core_ref[0] == 0
    left = jnp.concatenate([ref[...] for ref in parts], axis=1)
    rows = 64
    blocks = []
    for z in range(mine_ref.shape[0] // rows):
        mine, other = mine_ref[rows * z : rows * (z + 1)], other_ref[rows * z : rows * (z + 1)]
        blocks += [jnp.where(first, mine, other), jnp.where(first, other, mine)]
    total = lax.dot_general(left, jnp.concatenate(blocks, axis=0), NT, preferred_element_type=F32)
    side = math.isqrt(total.shape[0])
    half = side // 2
    for n, ref in enumerate(outs):
        start = side * half * (n // 2) + half * (n % 2)
        ref[...] = jnp.concatenate(
            [total[start + side * i : start + side * i + half] for i in range(half)], axis=0
        ).astype(BF)


def back_product(parts, mine, other, core):
    tokens = parts[0].shape[0]
    rows, inner = mine.shape
    steps = 4
    wide = 2 * rows // steps
    side = pl.BlockSpec((rows // steps, inner), lambda g: (g, 0))
    out = pl.BlockSpec((tokens // 4, wide), lambda g: (0, g))
    return pl.pallas_call(
        back_kernel,
        grid=(steps,),
        in_specs=[pl.BlockSpec(memory_space=pltpu.SMEM)]
        + [pl.BlockSpec(part.shape, lambda g: (0, 0)) for part in parts]
        + [side] * 2,
        out_specs=[out] * 4,
        out_shape=[shape(tokens // 4, wide * steps)(BF)] * 4,
        compiler_params=params(),
        cost_estimate=pl.CostEstimate(
            flops=6_000_000_000, bytes_accessed=12_000_000, transcendentals=0
        ),
        name="back_product",
    )(core, *parts, mine, other)


def position(row, col):
    return row // 2, row % 2 * 2 + col // 2, col % 2


def place(x, y, core):
    return x * 2 + y // 2, y % 2 * 2 + core


def block_order(row_count, col_count):
    order = []
    for core in range(2):
        for first in range(RADIX):
            for second in range(RADIX):
                x, y = (first, second) if core == 0 else (second, first)
                row, col = place(x, y, core)
                order.append(row * col_count + col)
    return order


def plane_pairs(rows, cols, turn, step):
    pairs = []
    for r in range(rows):
        for c in range(cols):
            x, y, core = position(r, c)
            if core == turn:
                x = (x + step) % RADIX
            else:
                y = (y + step) % RADIX
            to_r, to_c = place(x, y, core)
            pairs.append((r * cols + c, to_r * cols + to_c))
    return pairs


def round_pieces(total, gain, index, count):
    rows = total.shape[0] // count
    high = lax.reduce_precision(gain, 8, 7)
    low = lax.reduce_precision(gain - high, 8, 7)
    packed = pack_gain(high, low)
    pieces = [
        jnp.concatenate(
            [
                packed,
                lax.dynamic_slice_in_dim(total, (index + n) % count * rows, rows, 0).astype(BF),
            ],
            axis=0,
        )
        for n in range(1, count)
    ]
    return pieces, lax.dynamic_slice_in_dim(total, index * rows, rows, 0), high + low


def round_sums(got, own, gain, index):
    count = len(got) + 1
    gains = [gain]
    for value in got:
        own = own + value[GAIN_ROWS:].astype(F32)
        gains.append(value[0:1].astype(F32) + value[1:2].astype(F32))
    if count == 2:
        return own, gains[0] + gains[1]
    turned = jnp.concatenate(gains[::-1] * 2, axis=0)
    ordered = lax.dynamic_slice_in_dim(turned, count - 1 - index, count, 0)
    gain = ordered[0:1]
    for n in range(1, count):
        gain = gain + ordered[n : n + 1]
    return own, gain


def shift(value, rows, cols, step):
    r, c = lax.axis_size("row"), lax.axis_size("col")
    if rows and cols:
        pairs = [
            (i * c + j, (i + step) % r * c + (j + step) % c) for i in range(r) for j in range(c)
        ]
        return lax.ppermute(value, ("row", "col"), pairs)
    name, count = ("row", r) if rows else ("col", c)
    return lax.ppermute(value, name, [(i, (i + step) % count) for i in range(count)])


def quadrant(values, low_row, low_col):
    half = values.shape[0] // 2
    rows = slice(0, half) if low_row else slice(half, None)
    cols = slice(0, half) if low_col else slice(half, None)
    return values[rows, cols]


def per_device(qkv, grad_out, w_qkv, w_proj, norm_gain, region):
    side, width = grad_out.shape[1], grad_out.shape[3]
    half = side // 2
    tokens = side * side
    grad = grad_out[0]
    flat = (half * half, width)
    square = (half, half, width)

    def send(value, rows, cols, step):
        return shift(value.reshape(flat), rows, cols, step).reshape(square)

    core = lax.axis_index("col") % 2
    rows = w_qkv.shape[0] // 2
    mine_w = lax.dynamic_slice_in_dim(w_qkv, core * rows, rows, 0)
    mine = lax.all_gather(mine_w, "dp", axis=0, tiled=True)
    from_row = send(quadrant(grad, True, False), True, False, -1)
    from_col = send(quadrant(grad, False, True), False, True, -1)
    from_both = send(quadrant(grad, True, True), True, True, -1)

    ids = region.reshape(tokens, 1)
    lane = lax.broadcasted_iota(jnp.int32, (tokens, 128), 1)
    hot = (ids == lane % (width // HEADS)).astype(BF)
    qkv_t = qkv.reshape(tokens, 3 * width)
    groups = width // 128
    qkv_t, mine_w = lax.optimization_barrier((qkv_t, mine_w))
    probs, rest, out, inverse = forward(qkv_t, hot)

    dz = jnp.concatenate(
        [
            jnp.concatenate([quadrant(grad, False, False), from_col], axis=1),
            jnp.concatenate([from_row, from_both], axis=1),
        ],
        axis=0,
    ).reshape(tokens, width)

    r, c, d = lax.axis_size("row"), lax.axis_size("col"), lax.axis_size("dp")
    row, col, dp = lax.axis_index("row"), lax.axis_index("col"), lax.axis_index("dp")
    bit = core.astype(jnp.int32).reshape(1)
    dattn, wire, keep, gain = middle([out], w_proj, dz, norm_gain, bit, block_order(r, c))
    other = lax.ppermute(mine, "col", [(i, i ^ 1) for i in range(c)])
    norm = (tokens * r * c * d) ** (-0.5)
    got = lax.ppermute(wire, "col", [(i, i ^ 1) for i in range(c)])
    x, y, _ = position(row, col)

    def plane_round(pieces, turn):
        return [
            lax.ppermute(piece, ("row", "col"), plane_pairs(r, c, turn, n + 1))
            for n, piece in enumerate(pieces)
        ]

    def back_part(dattn, first, count):
        return backward(probs, rest, qkv_t, dattn, out, inverse, first, count)

    def halve(sums, gain, bit):
        index = dp // bit % 2
        (piece,), own, gain = round_pieces(sums, gain, index, 2)
        return piece, own, gain, index

    def swap(piece, bit):
        return lax.ppermute(piece, "dp", [(i, i ^ bit) for i in range(d)])

    first, second = groups // 4, groups // 4 + (groups - groups // 4) // 2
    part_a = back_part(dattn, 0, first)
    part_a, got = lax.optimization_barrier((part_a, got))
    sums = keep + got[GAIN_ROWS:].astype(F32)
    gain = gain + (got[0:1].astype(F32) + got[1:2].astype(F32))
    index = jnp.where(core == 0, x, y)
    pieces, own, gain = round_pieces(sums, gain, index, RADIX)
    dattn, pieces = lax.optimization_barrier((dattn, pieces))
    got = plane_round(pieces, 0)

    part_b = back_part(dattn, first, second - first)
    part_b, got = lax.optimization_barrier((part_b, got))
    sums, gain = round_sums(got, own, gain, index)
    index = jnp.where(core == 0, y, x)
    pieces, own, gain = round_pieces(sums, gain, index, RADIX)
    dattn, pieces = lax.optimization_barrier((dattn, pieces))
    got = plane_round(pieces, 1)

    part_c = back_part(dattn, second, groups - second)
    part_c, got = lax.optimization_barrier((part_c, got))
    sums, gain = round_sums(got, own, gain, index)
    piece, own, gain, index = halve(sums, gain, 4)
    part_c, piece = lax.optimization_barrier((part_c, piece))
    got = swap(piece, 4)

    parts = [part for trio in zip(part_a, part_b, part_c) for part in trio]
    quarters = back_product(parts, mine, other, bit)
    quarters, got = lax.optimization_barrier((quarters, got))
    local, to_col, to_row, to_both = [quarters[0]] + [
        shift(quarters[i], i // 2 == 1, i % 2 == 1, 1) for i in (1, 2, 3)
    ]
    sums, gain = round_sums([got], own, gain, index)
    piece, own, gain, index = halve(sums, gain, 2)
    sums, gain = round_sums([swap(piece, 2)], own, gain, index)
    sums, to_col = lax.optimization_barrier((sums, to_col))
    piece, own, gain, index = halve(sums, gain, 1)
    sums, gain = round_sums([swap(piece, 1)], own, gain, index)
    grad_proj, grad_gain = sums * norm, gain * norm

    local, to_col, to_row, to_both = (
        part.reshape(square) for part in (local, to_col, to_row, to_both)
    )
    moved = jnp.concatenate(
        [
            jnp.concatenate([to_both, to_row], axis=1),
            jnp.concatenate([to_col, local], axis=1),
        ],
        axis=0,
    )
    grad_in = (grad.astype(F32) + moved.astype(F32)).astype(BF)[None]
    return (grad_in, grad_proj, grad_gain[0])


def solution(mesh):
    return jax.shard_map(
        per_device,
        mesh=mesh,
        in_specs=(
            P("dp", "row", "col", None),
            P("dp", "row", "col", None),
            P("dp", None),
            P(),
            P(),
            P("row", "col"),
        ),
        out_specs=(P("dp", "row", "col", None), P(("row", "col", "dp"), None), P()),
        check_vma=False,
    )
```

```python
import math

import jax
import jax.numpy as jnp
from jax import lax
from jax.experimental import pallas as pl
from jax.experimental.pallas import tpu as pltpu
from jax.sharding import PartitionSpec as P

HEADS = 32
GROUP = 4
BF = jnp.bfloat16
F32 = jnp.float32
NT = (((1,), (1,)), ((), ()))
TN = (((0,), (0,)), ((), ()))
LIMIT = 56 * 2**20
GAIN_ROWS = 8
RADIX = 4
REGIONS = 4


def params():
    return pltpu.CompilerParams(vmem_limit_bytes=LIMIT)


def shape(*dims):
    return lambda kind: jax.ShapeDtypeStruct(dims, kind)


def split3(value):
    high = value.astype(BF)
    rest = value - high.astype(F32)
    mid = rest.astype(BF)
    return high, mid, (rest - mid.astype(F32)).astype(BF)


def by_head(parts):
    return jnp.concatenate(parts, axis=0)


def zero_unless(chosen, value):
    return jnp.where(chosen, value, jnp.zeros_like(value))


def forward_kernel(q_ref, k_ref, v_ref, hot_ref, p_ref, rest_ref, o_ref, inv_ref):
    tokens, lanes = q_ref.shape
    size = lanes // GROUP
    main = p_ref.shape[2]
    tail = tokens - main
    factor = size ** (-0.5) * math.log2(math.e)
    queries, keys, values, hot = q_ref[...], k_ref[...], v_ref[...], hot_ref[...]
    lane = lax.broadcasted_iota(jnp.int32, (tokens, lanes), 1)
    head = lane // size
    mask = jnp.where(lane % size < REGIONS, (hot.astype(F32) - 1.0) * 1e30, 0.0).astype(BF)
    tail_keys, tail_values, tail_head = keys[main:], values[main:], head[:tail]
    tail_mask = zero_unless(tail_head == 0, mask[main:])
    tail_scores = lax.dot_general(
        jnp.concatenate([queries, hot], axis=1),
        jnp.concatenate(
            [
                by_head([zero_unless(tail_head == h, tail_keys) for h in range(GROUP)]),
                by_head([tail_mask] * GROUP),
            ],
            axis=1,
        ),
        NT,
        preferred_element_type=F32,
    )
    per = lanes // tail
    main_head = head[:main]

    def scores_of(h):
        left = jnp.where(head == h, queries, hot)
        right = jnp.where(main_head == h, keys[:main], mask[:main])
        return lax.dot_general(left, right, NT, preferred_element_type=F32)

    scores = scores_of(0)
    last, sums, tops = None, [], []
    for h in range(GROUP + 1):
        ahead = scores_of(h + 1) if h + 1 < GROUP else None
        if last is not None:
            own = main_head == h - 1
            summed = jnp.where(own, values[:main], jnp.ones_like(values[:main]))
            sums.append(jnp.dot(last, summed, preferred_element_type=F32))
        if h < GROUP:
            tile = tail_scores[:, lanes * (h // per) : lanes * (h // per + 1)]
            top = jnp.where(lane // tail == h % per, tile, -3e38)
            for start in range(0, main, lanes):
                top = jnp.maximum(top, scores[:, start : start + lanes])
            tops.append(jnp.max(top, axis=1, keepdims=True))
            last = jnp.exp2((scores - tops[h]) * factor).astype(BF)
            p_ref[h] = last
        scores = ahead
    rest = []
    for n in range(GROUP // per):
        top = tops[n * per]
        for i in range(1, per):
            top = jnp.where(lane // tail == i, tops[n * per + i], top)
        tile = tail_scores[:, lanes * n : lanes * (n + 1)]
        rest.append(jnp.exp2((tile - top) * factor).astype(BF))
    rest = jnp.concatenate(rest, axis=1)
    rest_ref[...] = rest
    ones = jnp.ones_like(tail_values)
    right = by_head(
        [
            jnp.concatenate(
                [zero_unless(tail_head == h, tail_values), zero_unless(tail_head == h, ones)], axis=1
            )
            for h in range(GROUP)
        ]
    )
    both = jnp.dot(rest, right, preferred_element_type=F32)
    out, total = None, None
    for h, part in enumerate(sums):
        turned = pltpu.roll(part, size, axis=1)
        out = part if out is None else jnp.where(head == h, part, out)
        total = turned if total is None else jnp.where(head == h, turned, total)
    inverse = 1.0 / (total + both[:, lanes:])
    o_ref[...] = (out + both[:, :lanes]) * inverse
    inv_ref[...] = inverse


def backward_kernel(
    p_ref, rest_ref, q_ref, k_ref, v_ref, do_ref, o_ref, inv_ref, dq_ref, dk_ref, dv_ref
):
    tokens, lanes = q_ref.shape
    size = lanes // GROUP
    main = p_ref.shape[2]
    tail = tokens - main
    scale = size ** (-0.5)
    keys, values, dout, inv = k_ref[...], v_ref[...], do_ref[...], inv_ref[...]
    lane = lax.broadcasted_iota(jnp.int32, (tokens, lanes), 1)
    head, which = lane // size, lane % size
    dout_f = dout.astype(F32)
    row_i = lax.broadcasted_iota(jnp.int32, (lanes, lanes), 0) // size
    col_i = lax.broadcasted_iota(jnp.int32, (lanes, lanes), 1)
    pick = jnp.where((col_i // size == (row_i + 1) % GROUP) & (col_i % size < 3), 1.0, 0.0).astype(BF)
    parts = jnp.concatenate(split3(dout_f * o_ref[...]), axis=1)
    delta = jnp.dot(parts, jnp.concatenate([pick] * 3, axis=0), preferred_element_type=F32)
    d_high = delta.astype(BF).astype(F32)
    d_rest = delta - d_high
    d_mid = d_rest.astype(BF).astype(F32)
    columns = jnp.where(
        which == 0, d_high, jnp.where(which == 1, d_mid, jnp.where(which == 2, d_rest - d_mid, 0.0))
    ).astype(BF)
    dout_t = (dout_f * inv).T.astype(BF)
    query_t = (q_ref[...].astype(F32) * (inv * scale)).T.astype(BF)
    tail_head, main_head = head[:tail], head[:main]

    def minus(h, count):
        chosen = (head[:count] == (h + 1) % GROUP) & (which[:count] < 3)
        return jnp.where(chosen, -1.0, 0.0).astype(BF)

    rest = rest_ref[...]
    right = by_head(
        [
            jnp.concatenate([zero_unless(tail_head == h, values[main:]), minus(h, tail)], axis=1)
            for h in range(GROUP)
        ]
    )
    dprobs = lax.dot_general(
        jnp.concatenate([dout, columns], axis=1), right, NT, preferred_element_type=F32
    )
    dscores_rest = (rest.astype(F32) * dprobs).astype(BF)

    def dprobs_of(h):
        left = jnp.where(head == h, dout, columns)
        right = jnp.where(main_head == h, values[:main], minus(h, main))
        return lax.dot_general(left, right, NT, preferred_element_type=F32)

    dprobs = dprobs_of(0)
    dq, dks, dvs = None, [], []
    for h in range(GROUP):
        ahead = dprobs_of(h + 1) if h + 1 < GROUP else None
        probs = p_ref[h]
        dscores = (probs.astype(F32) * dprobs).astype(BF)
        part = jnp.dot(dscores, keys[:main], preferred_element_type=F32)
        dq = part if dq is None else jnp.where(head == h, part, dq)
        rows = slice(size * h, size * (h + 1))
        dks.append(jnp.dot(query_t[rows], dscores, preferred_element_type=F32))
        dvs.append(jnp.dot(dout_t[rows], probs, preferred_element_type=F32))
        dprobs = ahead
    right = by_head([zero_unless(tail_head == h, keys[main:]) for h in range(GROUP)])
    dq = dq + jnp.dot(dscores_rest, right, preferred_element_type=F32)
    dq_ref[...] = (dq * (inv * scale)).astype(BF)
    for ref, whole, left, right in (
        (dk_ref, dks, query_t, dscores_rest),
        (dv_ref, dvs, dout_t, rest),
    ):
        ref[0:main] = jnp.concatenate(whole, axis=0).T.astype(BF)
        turned = jnp.dot(left, right, preferred_element_type=F32).T
        last = turned[0:tail]
        for h in range(1, GROUP):
            last = jnp.where(tail_head == h, turned[tail * h : tail * (h + 1)], last)
        ref[main:] = last.astype(BF)


def column_block(tokens, offset):
    return pl.BlockSpec((tokens, 128), lambda g: (0, g + offset))


def forward(qkv, hot):
    tokens = qkv.shape[0]
    per = qkv.shape[1] // 3 // 128
    main = tokens // 256 * 256
    rest = (tokens - main) * GROUP
    out = shape(tokens, per * 128)(F32)
    return pl.pallas_call(
        forward_kernel,
        grid=(per,),
        in_specs=[column_block(tokens, per * i) for i in range(3)]
        + [pl.BlockSpec((tokens, 128), lambda g: (0, 0))],
        out_specs=[
            pl.BlockSpec((GROUP, tokens, main), lambda g: (g, 0, 0)),
            pl.BlockSpec((tokens, rest), lambda g: (0, g)),
        ]
        + [column_block(tokens, 0)] * 2,
        out_shape=[
            shape(per * GROUP, tokens, main)(BF),
            shape(tokens, per * rest)(BF),
            out,
            out,
        ],
        compiler_params=params(),
        cost_estimate=pl.CostEstimate(
            flops=per * 3_200_000_000, bytes_accessed=per * 4_000_000, transcendentals=0
        ),
        name="attn_forward",
    )(qkv, qkv, qkv, hot)


def backward(probs, rest, qkv, dattn, out, inverse, first, count):
    tokens = qkv.shape[0]
    per = qkv.shape[1] // 3 // 128
    return pl.pallas_call(
        backward_kernel,
        grid=(count,),
        in_specs=[
            pl.BlockSpec((GROUP, *probs.shape[1:]), lambda g: (g + first, 0, 0)),
            pl.BlockSpec((tokens, rest.shape[1] // per), lambda g: (0, g + first)),
        ]
        + [column_block(tokens, first + per * i) for i in range(3)]
        + [column_block(tokens, first)] * 3,
        out_specs=[column_block(tokens, 0)] * 3,
        out_shape=[shape(tokens, count * 128)(BF)] * 3,
        compiler_params=params(),
        cost_estimate=pl.CostEstimate(
            flops=count * 3_600_000_000, bytes_accessed=count * 4_000_000, transcendentals=0
        ),
        name="attn_backward",
    )(probs, rest, qkv, qkv, qkv, dattn, out, inverse)


def pack_gain(high, low):
    rows = lax.broadcasted_iota(jnp.int32, (GAIN_ROWS, high.shape[1]), 0)
    return jnp.where(rows == 0, high, jnp.where(rows == 1, low, 0.0)).astype(BF)


def middle_kernel(order, bit_ref, *refs):
    outs, (w_ref, dz_ref, gain_ref, do_ref, send_ref, keep_ref, term_ref, sums) = refs[:-8], refs[-8:]
    attn = jnp.concatenate([ref[...].astype(BF) for ref in outs], axis=1)
    weights = w_ref[...]
    proj = jnp.dot(attn, weights, preferred_element_type=F32)
    centred = proj - jnp.mean(proj, axis=1, keepdims=True)
    rstd = lax.rsqrt(jnp.mean(centred * centred, axis=1, keepdims=True) + 1e-05)
    normed = centred * rstd
    dz = dz_ref[...].astype(F32)
    term = jnp.sum(dz * normed, axis=0, keepdims=True)
    scaled = dz * gain_ref[...]
    mean = jnp.mean(scaled, axis=1, keepdims=True)
    dot = jnp.mean(scaled * normed, axis=1, keepdims=True)
    dproj = (rstd * (scaled - mean - normed * dot)).astype(BF)
    do_ref[...] = lax.dot_general(dproj, weights, NT, preferred_element_type=F32).astype(BF)
    sums[...] = lax.dot_general(attn, dproj, TN, preferred_element_type=F32)
    half = len(order) // 2
    size = sums.shape[0] // len(order)
    low, high = (
        jnp.concatenate([sums[size * b : size * (b + 1)] for b in part], axis=0)
        for part in (order[:half], order[half:])
    )
    second = bit_ref[0] == 1
    term_high = term.astype(BF).astype(F32)
    term_low = (term - term_high).astype(BF).astype(F32)
    send_ref[0:GAIN_ROWS] = pack_gain(term_high, term_low)
    send_ref[GAIN_ROWS:] = jnp.where(second, low, high).astype(BF)
    keep_ref[...] = jnp.where(second, high, low)
    term_ref[...] = term_high + term_low


def middle(outs, w_proj, dz, gain, bit, order):
    tokens, width = dz.shape
    vmem = pl.BlockSpec(memory_space=pltpu.VMEM)
    half = width // 2
    return pl.pallas_call(
        lambda *refs: middle_kernel(order, *refs),
        in_specs=[pl.BlockSpec(memory_space=pltpu.SMEM)] + [vmem] * (len(outs) + 3),
        out_specs=[vmem] * 4,
        out_shape=[
            shape(tokens, width)(BF),
            shape(GAIN_ROWS + half, width)(BF),
            shape(half, width)(F32),
            shape(1, width)(F32),
        ],
        scratch_shapes=[pltpu.VMEM((width, width), F32)],
        compiler_params=params(),
        cost_estimate=pl.CostEstimate(
            flops=8_000_000_000, bytes_accessed=16_000_000, transcendentals=0
        ),
        name="middle",
    )(bit, *outs, w_proj, dz, gain[None])


def back_kernel(core_ref, *refs):
    parts, (mine_ref, other_ref), outs = refs[:-6], refs[-6:-4], refs[-4:]
    first = core_ref[0] == 0
    left = jnp.concatenate([ref[...] for ref in parts], axis=1)
    rows = 64
    blocks = []
    for z in range(mine_ref.shape[0] // rows):
        mine, other = mine_ref[rows * z : rows * (z + 1)], other_ref[rows * z : rows * (z + 1)]
        blocks += [jnp.where(first, mine, other), jnp.where(first, other, mine)]
    total = lax.dot_general(left, jnp.concatenate(blocks, axis=0), NT, preferred_element_type=F32)
    side = math.isqrt(total.shape[0])
    half = side // 2
    for n, ref in enumerate(outs):
        start = side * half * (n // 2) + half * (n % 2)
        ref[...] = jnp.concatenate(
            [total[start + side * i : start + side * i + half] for i in range(half)], axis=0
        ).astype(BF)


def back_product(parts, mine, other, core, which):
    tokens = parts[0].shape[0]
    rows, inner = mine.shape
    steps = 2
    wide = 2 * rows // (2 * steps)
    side = pl.BlockSpec((rows // (2 * steps), inner), lambda g: (g + which * steps, 0))
    out = pl.BlockSpec((tokens // 4, wide), lambda g: (0, g))
    return pl.pallas_call(
        back_kernel,
        grid=(steps,),
        in_specs=[pl.BlockSpec(memory_space=pltpu.SMEM)]
        + [pl.BlockSpec(part.shape, lambda g: (0, 0)) for part in parts]
        + [side] * 2,
        out_specs=[out] * 4,
        out_shape=[shape(tokens // 4, wide * steps)(BF)] * 4,
        compiler_params=params(),
        cost_estimate=pl.CostEstimate(
            flops=3_000_000_000, bytes_accessed=8_000_000, transcendentals=0
        ),
        name="back_product",
    )(core, *parts, mine, other)


def position(row, col):
    return row // 2, row % 2 * 2 + col // 2, col % 2


def place(x, y, core):
    return x * 2 + y // 2, y % 2 * 2 + core


def block_order(row_count, col_count):
    order = []
    for core in range(2):
        for first in range(RADIX):
            for second in range(RADIX):
                x, y = (first, second) if core == 0 else (second, first)
                row, col = place(x, y, core)
                order.append(row * col_count + col)
    return order


def plane_pairs(rows, cols, turn, step):
    pairs = []
    for r in range(rows):
        for c in range(cols):
            x, y, core = position(r, c)
            if core == turn:
                x = (x + step) % RADIX
            else:
                y = (y + step) % RADIX
            to_r, to_c = place(x, y, core)
            pairs.append((r * cols + c, to_r * cols + to_c))
    return pairs


def round_pieces(total, gain, index, count):
    rows = total.shape[0] // count
    high = lax.reduce_precision(gain, 8, 7)
    low = lax.reduce_precision(gain - high, 8, 7)
    packed = pack_gain(high, low)
    pieces = [
        jnp.concatenate(
            [
                packed,
                lax.dynamic_slice_in_dim(total, (index + n) % count * rows, rows, 0).astype(BF),
            ],
            axis=0,
        )
        for n in range(1, count)
    ]
    return pieces, lax.dynamic_slice_in_dim(total, index * rows, rows, 0), high + low


def round_sums(got, own, gain, index):
    count = len(got) + 1
    gains = [gain]
    for value in got:
        own = own + value[GAIN_ROWS:].astype(F32)
        gains.append(value[0:1].astype(F32) + value[1:2].astype(F32))
    if count == 2:
        return own, gains[0] + gains[1]
    turned = jnp.concatenate(gains[::-1] * 2, axis=0)
    ordered = lax.dynamic_slice_in_dim(turned, count - 1 - index, count, 0)
    gain = ordered[0:1]
    for n in range(1, count):
        gain = gain + ordered[n : n + 1]
    return own, gain


def shift(value, rows, cols, step):
    r, c = lax.axis_size("row"), lax.axis_size("col")
    if rows and cols:
        pairs = [
            (i * c + j, (i + step) % r * c + (j + step) % c) for i in range(r) for j in range(c)
        ]
        return lax.ppermute(value, ("row", "col"), pairs)
    name, count = ("row", r) if rows else ("col", c)
    return lax.ppermute(value, name, [(i, (i + step) % count) for i in range(count)])


def quadrant(values, low_row, low_col):
    half = values.shape[0] // 2
    rows = slice(0, half) if low_row else slice(half, None)
    cols = slice(0, half) if low_col else slice(half, None)
    return values[rows, cols]


def per_device(qkv, grad_out, w_qkv, w_proj, norm_gain, region):
    side, width = grad_out.shape[1], grad_out.shape[3]
    half = side // 2
    tokens = side * side
    grad = grad_out[0]
    flat = (half * half, width)
    square = (half, half, width)

    def send(value, rows, cols, step):
        return shift(value.reshape(flat), rows, cols, step).reshape(square)

    core = lax.axis_index("col") % 2
    rows = w_qkv.shape[0] // 2
    mine_w = lax.dynamic_slice_in_dim(w_qkv, core * rows, rows, 0)
    mine = lax.all_gather(mine_w, "dp", axis=0, tiled=True)
    from_row = send(quadrant(grad, True, False), True, False, -1)
    from_col = send(quadrant(grad, False, True), False, True, -1)
    from_both = send(quadrant(grad, True, True), True, True, -1)

    ids = region.reshape(tokens, 1)
    lane = lax.broadcasted_iota(jnp.int32, (tokens, 128), 1)
    hot = (ids == lane % (width // HEADS)).astype(BF)
    qkv_t = qkv.reshape(tokens, 3 * width)
    groups = width // 128
    qkv_t, mine_w = lax.optimization_barrier((qkv_t, mine_w))
    probs, rest, out, inverse = forward(qkv_t, hot)

    dz = jnp.concatenate(
        [
            jnp.concatenate([quadrant(grad, False, False), from_col], axis=1),
            jnp.concatenate([from_row, from_both], axis=1),
        ],
        axis=0,
    ).reshape(tokens, width)

    r, c, d = lax.axis_size("row"), lax.axis_size("col"), lax.axis_size("dp")
    row, col, dp = lax.axis_index("row"), lax.axis_index("col"), lax.axis_index("dp")
    bit = core.astype(jnp.int32).reshape(1)
    dattn, wire, keep, gain = middle([out], w_proj, dz, norm_gain, bit, block_order(r, c))
    other = lax.ppermute(mine, "col", [(i, i ^ 1) for i in range(c)])
    norm = (tokens * r * c * d) ** (-0.5)
    got = lax.ppermute(wire, "col", [(i, i ^ 1) for i in range(c)])
    x, y, _ = position(row, col)

    def plane_round(pieces, turn):
        return [
            lax.ppermute(piece, ("row", "col"), plane_pairs(r, c, turn, n + 1))
            for n, piece in enumerate(pieces)
        ]

    def back_part(dattn, first, count):
        return backward(probs, rest, qkv_t, dattn, out, inverse, first, count)

    def halve(sums, gain, bit):
        index = dp // bit % 2
        (piece,), own, gain = round_pieces(sums, gain, index, 2)
        return piece, own, gain, index

    def swap(piece, bit):
        return lax.ppermute(piece, "dp", [(i, i ^ bit) for i in range(d)])

    first, second = groups // 4, groups // 4 + (groups - groups // 4) // 2
    part_a = back_part(dattn, 0, first)
    part_a, got = lax.optimization_barrier((part_a, got))
    sums = keep + got[GAIN_ROWS:].astype(F32)
    gain = gain + (got[0:1].astype(F32) + got[1:2].astype(F32))
    index = jnp.where(core == 0, x, y)
    pieces, own, gain = round_pieces(sums, gain, index, RADIX)
    dattn, pieces = lax.optimization_barrier((dattn, pieces))
    got = plane_round(pieces, 0)

    part_b = back_part(dattn, first, second - first)
    part_b, got = lax.optimization_barrier((part_b, got))
    sums, gain = round_sums(got, own, gain, index)
    index = jnp.where(core == 0, y, x)
    pieces, own, gain = round_pieces(sums, gain, index, RADIX)
    dattn, pieces = lax.optimization_barrier((dattn, pieces))
    got = plane_round(pieces, 1)

    part_c = back_part(dattn, second, groups - second)
    part_c, got = lax.optimization_barrier((part_c, got))
    sums, gain = round_sums(got, own, gain, index)
    piece, own, gain, index = halve(sums, gain, 4)
    part_c, piece = lax.optimization_barrier((part_c, piece))
    got = swap(piece, 4)

    parts = [part for trio in zip(part_a, part_b, part_c) for part in trio]
    def halos(quarters):
        return [quarters[0]] + [
            shift(quarters[i], i // 2 == 1, i % 2 == 1, 1) for i in (1, 2, 3)
        ]

    quarters = back_product(parts, mine, other, bit, 0)
    quarters, got = lax.optimization_barrier((quarters, got))
    moved = [halos(quarters)]
    sums, gain = round_sums([got], own, gain, index)
    piece, own, gain, index = halve(sums, gain, 2)
    parts, piece = lax.optimization_barrier((parts, piece))
    got = swap(piece, 2)
    quarters = back_product(parts, mine, other, bit, 1)
    quarters, got, moved[0][2:] = lax.optimization_barrier((quarters, got, moved[0][2:]))
    moved.append(halos(quarters))
    sums, gain = round_sums([got], own, gain, index)
    piece, own, gain, index = halve(sums, gain, 1)
    sums, gain = round_sums([swap(piece, 1)], own, gain, index)
    grad_proj, grad_gain = sums * norm, gain * norm
    grad_proj, grad_gain, moved[1] = lax.optimization_barrier((grad_proj, grad_gain, moved[1]))

    local, to_col, to_row, to_both = (
        jnp.concatenate(pair, axis=1).reshape(square) for pair in zip(*moved)
    )
    moved = jnp.concatenate(
        [
            jnp.concatenate([to_both, to_row], axis=1),
            jnp.concatenate([to_col, local], axis=1),
        ],
        axis=0,
    )
    grad_in = (grad.astype(F32) + moved.astype(F32)).astype(BF)[None]
    return (grad_in, grad_proj, grad_gain[0])


def solution(mesh):
    return jax.shard_map(
        per_device,
        mesh=mesh,
        in_specs=(
            P("dp", "row", "col", None),
            P("dp", "row", "col", None),
            P("dp", None),
            P(),
            P(),
            P("row", "col"),
        ),
        out_specs=(P("dp", "row", "col", None), P(("row", "col", "dp"), None), P()),
        check_vma=False,
    )
```

```python
import math

import jax
import jax.numpy as jnp
from jax import lax
from jax.experimental import pallas as pl
from jax.experimental.pallas import tpu as pltpu
from jax.sharding import PartitionSpec as P

HEADS = 32
GROUP = 4
BF = jnp.bfloat16
F32 = jnp.float32
NT = (((1,), (1,)), ((), ()))
TN = (((0,), (0,)), ((), ()))
LIMIT = 56 * 2**20
GAIN_ROWS = 8
RADIX = 4
REGIONS = 4


def params():
    return pltpu.CompilerParams(vmem_limit_bytes=LIMIT)


def shape(*dims):
    return lambda kind: jax.ShapeDtypeStruct(dims, kind)


def split3(value):
    high = value.astype(BF)
    rest = value - high.astype(F32)
    mid = rest.astype(BF)
    return high, mid, (rest - mid.astype(F32)).astype(BF)


def by_head(parts):
    return jnp.concatenate(parts, axis=0)


def zero_unless(chosen, value):
    return jnp.where(chosen, value, jnp.zeros_like(value))


def forward_kernel(q_ref, k_ref, v_ref, hot_ref, p_ref, rest_ref, o_ref, inv_ref):
    tokens, lanes = q_ref.shape
    size = lanes // GROUP
    main = p_ref.shape[2]
    tail = tokens - main
    factor = size ** (-0.5) * math.log2(math.e)
    queries, keys, values, hot = q_ref[...], k_ref[...], v_ref[...], hot_ref[...]
    lane = lax.broadcasted_iota(jnp.int32, (tokens, lanes), 1)
    head = lane // size
    mask = jnp.where(lane % size < REGIONS, (hot.astype(F32) - 1.0) * 1e30, 0.0).astype(BF)
    tail_keys, tail_values, tail_head = keys[main:], values[main:], head[:tail]
    tail_mask = zero_unless(tail_head == 0, mask[main:])
    tail_scores = lax.dot_general(
        jnp.concatenate([queries, hot], axis=1),
        jnp.concatenate(
            [
                by_head([zero_unless(tail_head == h, tail_keys) for h in range(GROUP)]),
                by_head([tail_mask] * GROUP),
            ],
            axis=1,
        ),
        NT,
        preferred_element_type=F32,
    )
    per = lanes // tail
    main_head = head[:main]

    def scores_of(h):
        left = jnp.where(head == h, queries, hot)
        right = jnp.where(main_head == h, keys[:main], mask[:main])
        return lax.dot_general(left, right, NT, preferred_element_type=F32)

    scores = scores_of(0)
    last, sums, tops = None, [], []
    for h in range(GROUP + 1):
        ahead = scores_of(h + 1) if h + 1 < GROUP else None
        if last is not None:
            own = main_head == h - 1
            summed = jnp.where(own, values[:main], jnp.ones_like(values[:main]))
            sums.append(jnp.dot(last, summed, preferred_element_type=F32))
        if h < GROUP:
            tile = tail_scores[:, lanes * (h // per) : lanes * (h // per + 1)]
            top = jnp.where(lane // tail == h % per, tile, -3e38)
            for start in range(0, main, lanes):
                top = jnp.maximum(top, scores[:, start : start + lanes])
            tops.append(jnp.max(top, axis=1, keepdims=True))
            last = jnp.exp2((scores - tops[h]) * factor).astype(BF)
            p_ref[h] = last
        scores = ahead
    rest = []
    for n in range(GROUP // per):
        top = tops[n * per]
        for i in range(1, per):
            top = jnp.where(lane // tail == i, tops[n * per + i], top)
        tile = tail_scores[:, lanes * n : lanes * (n + 1)]
        rest.append(jnp.exp2((tile - top) * factor).astype(BF))
    rest = jnp.concatenate(rest, axis=1)
    rest_ref[...] = rest
    ones = jnp.ones_like(tail_values)
    right = by_head(
        [
            jnp.concatenate(
                [zero_unless(tail_head == h, tail_values), zero_unless(tail_head == h, ones)], axis=1
            )
            for h in range(GROUP)
        ]
    )
    both = jnp.dot(rest, right, preferred_element_type=F32)
    out, total = None, None
    for h, part in enumerate(sums):
        turned = pltpu.roll(part, size, axis=1)
        out = part if out is None else jnp.where(head == h, part, out)
        total = turned if total is None else jnp.where(head == h, turned, total)
    inverse = 1.0 / (total + both[:, lanes:])
    o_ref[...] = (out + both[:, :lanes]) * inverse
    inv_ref[...] = inverse


def backward_kernel(
    p_ref, rest_ref, q_ref, k_ref, v_ref, do_ref, o_ref, inv_ref, dq_ref, dk_ref, dv_ref
):
    tokens, lanes = q_ref.shape
    size = lanes // GROUP
    main = p_ref.shape[2]
    tail = tokens - main
    scale = size ** (-0.5)
    keys, values, dout, inv = k_ref[...], v_ref[...], do_ref[...], inv_ref[...]
    lane = lax.broadcasted_iota(jnp.int32, (tokens, lanes), 1)
    head, which = lane // size, lane % size
    dout_f = dout.astype(F32)
    row_i = lax.broadcasted_iota(jnp.int32, (lanes, lanes), 0) // size
    col_i = lax.broadcasted_iota(jnp.int32, (lanes, lanes), 1)
    pick = jnp.where((col_i // size == (row_i + 1) % GROUP) & (col_i % size < 3), 1.0, 0.0).astype(BF)
    parts = jnp.concatenate(split3(dout_f * o_ref[...]), axis=1)
    delta = jnp.dot(parts, jnp.concatenate([pick] * 3, axis=0), preferred_element_type=F32)
    d_high = delta.astype(BF).astype(F32)
    d_rest = delta - d_high
    d_mid = d_rest.astype(BF).astype(F32)
    columns = jnp.where(
        which == 0, d_high, jnp.where(which == 1, d_mid, jnp.where(which == 2, d_rest - d_mid, 0.0))
    ).astype(BF)
    dout_t = (dout_f * inv).T.astype(BF)
    query_t = (q_ref[...].astype(F32) * (inv * scale)).T.astype(BF)
    tail_head, main_head = head[:tail], head[:main]

    def minus(h, count):
        chosen = (head[:count] == (h + 1) % GROUP) & (which[:count] < 3)
        return jnp.where(chosen, -1.0, 0.0).astype(BF)

    rest = rest_ref[...]
    right = by_head(
        [
            jnp.concatenate([zero_unless(tail_head == h, values[main:]), minus(h, tail)], axis=1)
            for h in range(GROUP)
        ]
    )
    dprobs = lax.dot_general(
        jnp.concatenate([dout, columns], axis=1), right, NT, preferred_element_type=F32
    )
    dscores_rest = (rest.astype(F32) * dprobs).astype(BF)

    def dprobs_of(h):
        left = jnp.where(head == h, dout, columns)
        right = jnp.where(main_head == h, values[:main], minus(h, main))
        return lax.dot_general(left, right, NT, preferred_element_type=F32)

    dprobs = dprobs_of(0)
    dq, dks, dvs = None, [], []
    for h in range(GROUP):
        ahead = dprobs_of(h + 1) if h + 1 < GROUP else None
        probs = p_ref[h]
        dscores = (probs.astype(F32) * dprobs).astype(BF)
        part = jnp.dot(dscores, keys[:main], preferred_element_type=F32)
        dq = part if dq is None else jnp.where(head == h, part, dq)
        rows = slice(size * h, size * (h + 1))
        dks.append(jnp.dot(query_t[rows], dscores, preferred_element_type=F32))
        dvs.append(jnp.dot(dout_t[rows], probs, preferred_element_type=F32))
        dprobs = ahead
    right = by_head([zero_unless(tail_head == h, keys[main:]) for h in range(GROUP)])
    dq = dq + jnp.dot(dscores_rest, right, preferred_element_type=F32)
    dq_ref[...] = (dq * (inv * scale)).astype(BF)
    for ref, whole, left, right in (
        (dk_ref, dks, query_t, dscores_rest),
        (dv_ref, dvs, dout_t, rest),
    ):
        ref[0:main] = jnp.concatenate(whole, axis=0).T.astype(BF)
        turned = jnp.dot(left, right, preferred_element_type=F32).T
        last = turned[0:tail]
        for h in range(1, GROUP):
            last = jnp.where(tail_head == h, turned[tail * h : tail * (h + 1)], last)
        ref[main:] = last.astype(BF)


def column_block(tokens, offset):
    return pl.BlockSpec((tokens, 128), lambda g: (0, g + offset))


def forward(qkv, hot):
    tokens = qkv.shape[0]
    per = qkv.shape[1] // 3 // 128
    main = tokens // 256 * 256
    rest = (tokens - main) * GROUP
    out = shape(tokens, per * 128)(F32)
    return pl.pallas_call(
        forward_kernel,
        grid=(per,),
        in_specs=[column_block(tokens, per * i) for i in range(3)]
        + [pl.BlockSpec((tokens, 128), lambda g: (0, 0))],
        out_specs=[
            pl.BlockSpec((GROUP, tokens, main), lambda g: (g, 0, 0)),
            pl.BlockSpec((tokens, rest), lambda g: (0, g)),
        ]
        + [column_block(tokens, 0)] * 2,
        out_shape=[
            shape(per * GROUP, tokens, main)(BF),
            shape(tokens, per * rest)(BF),
            out,
            out,
        ],
        compiler_params=params(),
        cost_estimate=pl.CostEstimate(
            flops=per * 3_200_000_000, bytes_accessed=per * 4_000_000, transcendentals=0
        ),
        name="attn_forward",
    )(qkv, qkv, qkv, hot)


def backward(probs, rest, qkv, dattn, out, inverse, first, count):
    tokens = qkv.shape[0]
    per = qkv.shape[1] // 3 // 128
    return pl.pallas_call(
        backward_kernel,
        grid=(count,),
        in_specs=[
            pl.BlockSpec((GROUP, *probs.shape[1:]), lambda g: (g + first, 0, 0)),
            pl.BlockSpec((tokens, rest.shape[1] // per), lambda g: (0, g + first)),
        ]
        + [column_block(tokens, first + per * i) for i in range(3)]
        + [column_block(tokens, first)] * 3,
        out_specs=[column_block(tokens, 0)] * 3,
        out_shape=[shape(tokens, count * 128)(BF)] * 3,
        compiler_params=params(),
        cost_estimate=pl.CostEstimate(
            flops=count * 3_600_000_000, bytes_accessed=count * 4_000_000, transcendentals=0
        ),
        name="attn_backward",
    )(probs, rest, qkv, qkv, qkv, dattn, out, inverse)


def pack_gain(high, low):
    rows = lax.broadcasted_iota(jnp.int32, (GAIN_ROWS, high.shape[1]), 0)
    return jnp.where(rows == 0, high, jnp.where(rows == 1, low, 0.0)).astype(BF)


def middle_kernel(order, bit_ref, *refs):
    outs, (w_ref, dz_ref, gain_ref, do_ref, send_ref, keep_ref, term_ref, sums) = refs[:-8], refs[-8:]
    attn = jnp.concatenate([ref[...].astype(BF) for ref in outs], axis=1)
    weights = w_ref[...]
    proj = jnp.dot(attn, weights, preferred_element_type=F32)
    centred = proj - jnp.mean(proj, axis=1, keepdims=True)
    rstd = lax.rsqrt(jnp.mean(centred * centred, axis=1, keepdims=True) + 1e-05)
    normed = centred * rstd
    dz = dz_ref[...].astype(F32)
    term = jnp.sum(dz * normed, axis=0, keepdims=True)
    scaled = dz * gain_ref[...]
    mean = jnp.mean(scaled, axis=1, keepdims=True)
    dot = jnp.mean(scaled * normed, axis=1, keepdims=True)
    dproj = (rstd * (scaled - mean - normed * dot)).astype(BF)
    do_ref[...] = lax.dot_general(dproj, weights, NT, preferred_element_type=F32).astype(BF)
    sums[...] = lax.dot_general(attn, dproj, TN, preferred_element_type=F32)
    half = len(order) // 2
    size = sums.shape[0] // len(order)
    low, high = (
        jnp.concatenate([sums[size * b : size * (b + 1)] for b in part], axis=0)
        for part in (order[:half], order[half:])
    )
    second = bit_ref[0] == 1
    term_high = term.astype(BF).astype(F32)
    term_low = (term - term_high).astype(BF).astype(F32)
    send_ref[0:GAIN_ROWS] = pack_gain(term_high, term_low)
    send_ref[GAIN_ROWS:] = jnp.where(second, low, high).astype(BF)
    keep_ref[...] = jnp.where(second, high, low)
    term_ref[...] = term_high + term_low


def middle(outs, w_proj, dz, gain, bit, order):
    tokens, width = dz.shape
    vmem = pl.BlockSpec(memory_space=pltpu.VMEM)
    half = width // 2
    return pl.pallas_call(
        lambda *refs: middle_kernel(order, *refs),
        in_specs=[pl.BlockSpec(memory_space=pltpu.SMEM)] + [vmem] * (len(outs) + 3),
        out_specs=[vmem] * 4,
        out_shape=[
            shape(tokens, width)(BF),
            shape(GAIN_ROWS + half, width)(BF),
            shape(half, width)(F32),
            shape(1, width)(F32),
        ],
        scratch_shapes=[pltpu.VMEM((width, width), F32)],
        compiler_params=params(),
        cost_estimate=pl.CostEstimate(
            flops=8_000_000_000, bytes_accessed=16_000_000, transcendentals=0
        ),
        name="middle",
    )(bit, *outs, w_proj, dz, gain[None])


def back_kernel(core_ref, *refs):
    parts, (mine_ref, other_ref), outs = refs[:-6], refs[-6:-4], refs[-4:]
    first = core_ref[0] == 0
    left = jnp.concatenate([ref[...] for ref in parts], axis=1)
    rows = 64
    blocks = []
    for z in range(mine_ref.shape[0] // rows):
        mine, other = mine_ref[rows * z : rows * (z + 1)], other_ref[rows * z : rows * (z + 1)]
        blocks += [jnp.where(first, mine, other), jnp.where(first, other, mine)]
    total = lax.dot_general(left, jnp.concatenate(blocks, axis=0), NT, preferred_element_type=F32)
    side = math.isqrt(total.shape[0])
    half = side // 2
    for n, ref in enumerate(outs):
        start = side * half * (n // 2) + half * (n % 2)
        ref[...] = jnp.concatenate(
            [total[start + side * i : start + side * i + half] for i in range(half)], axis=0
        ).astype(BF)


def back_product(parts, mine, other, core):
    tokens = parts[0].shape[0]
    rows, inner = mine.shape
    steps = 4
    wide = 2 * rows // steps
    side = pl.BlockSpec((rows // steps, inner), lambda g: (g, 0))
    out = pl.BlockSpec((tokens // 4, wide), lambda g: (0, g))
    return pl.pallas_call(
        back_kernel,
        grid=(steps,),
        in_specs=[pl.BlockSpec(memory_space=pltpu.SMEM)]
        + [pl.BlockSpec(part.shape, lambda g: (0, 0)) for part in parts]
        + [side] * 2,
        out_specs=[out] * 4,
        out_shape=[shape(tokens // 4, wide * steps)(BF)] * 4,
        compiler_params=params(),
        cost_estimate=pl.CostEstimate(
            flops=6_000_000_000, bytes_accessed=12_000_000, transcendentals=0
        ),
        name="back_product",
    )(core, *parts, mine, other)


def position(row, col):
    return row // 2, row % 2 * 2 + col // 2, col % 2


def place(x, y, core):
    return x * 2 + y // 2, y % 2 * 2 + core


def block_order(row_count, col_count):
    order = []
    for core in range(2):
        for first in range(RADIX):
            for second in range(RADIX):
                x, y = (first, second) if core == 0 else (second, first)
                row, col = place(x, y, core)
                order.append(row * col_count + col)
    return order


def plane_pairs(rows, cols, turn, step):
    pairs = []
    for r in range(rows):
        for c in range(cols):
            x, y, core = position(r, c)
            if core == turn:
                x = (x + step) % RADIX
            else:
                y = (y + step) % RADIX
            to_r, to_c = place(x, y, core)
            pairs.append((r * cols + c, to_r * cols + to_c))
    return pairs


def round_pieces(total, gain, index, count):
    rows = total.shape[0] // count
    high = lax.reduce_precision(gain, 8, 7)
    low = lax.reduce_precision(gain - high, 8, 7)
    packed = pack_gain(high, low)
    pieces = [
        jnp.concatenate(
            [
                packed,
                lax.dynamic_slice_in_dim(total, (index + n) % count * rows, rows, 0).astype(BF),
            ],
            axis=0,
        )
        for n in range(1, count)
    ]
    return pieces, lax.dynamic_slice_in_dim(total, index * rows, rows, 0), high + low


def round_sums(got, own, gain, index):
    count = len(got) + 1
    gains = [gain]
    for value in got:
        own = own + value[GAIN_ROWS:].astype(F32)
        gains.append(value[0:1].astype(F32) + value[1:2].astype(F32))
    if count == 2:
        return own, gains[0] + gains[1]
    turned = jnp.concatenate(gains[::-1] * 2, axis=0)
    ordered = lax.dynamic_slice_in_dim(turned, count - 1 - index, count, 0)
    gain = ordered[0:1]
    for n in range(1, count):
        gain = gain + ordered[n : n + 1]
    return own, gain


def shift(value, rows, cols, step):
    r, c = lax.axis_size("row"), lax.axis_size("col")
    if rows and cols:
        pairs = [
            (i * c + j, (i + step) % r * c + (j + step) % c) for i in range(r) for j in range(c)
        ]
        return lax.ppermute(value, ("row", "col"), pairs)
    name, count = ("row", r) if rows else ("col", c)
    return lax.ppermute(value, name, [(i, (i + step) % count) for i in range(count)])


def quadrant(values, low_row, low_col):
    half = values.shape[0] // 2
    rows = slice(0, half) if low_row else slice(half, None)
    cols = slice(0, half) if low_col else slice(half, None)
    return values[rows, cols]


def per_device(qkv, grad_out, w_qkv, w_proj, norm_gain, region):
    side, width = grad_out.shape[1], grad_out.shape[3]
    half = side // 2
    tokens = side * side
    grad = grad_out[0]
    flat = (half * half, width)
    square = (half, half, width)

    def send(value, rows, cols, step):
        return shift(value.reshape(flat), rows, cols, step).reshape(square)

    core = lax.axis_index("col") % 2
    rows = w_qkv.shape[0] // 2
    mine_w = lax.dynamic_slice_in_dim(w_qkv, core * rows, rows, 0)
    mine = lax.all_gather(mine_w, "dp", axis=0, tiled=True)
    from_row = send(quadrant(grad, True, False), True, False, -1)
    from_col = send(quadrant(grad, False, True), False, True, -1)
    from_both = send(quadrant(grad, True, True), True, True, -1)

    ids = region.reshape(tokens, 1)
    lane = lax.broadcasted_iota(jnp.int32, (tokens, 128), 1)
    hot = (ids == lane % (width // HEADS)).astype(BF)
    qkv_t = qkv.reshape(tokens, 3 * width)
    groups = width // 128
    qkv_t, mine_w = lax.optimization_barrier((qkv_t, mine_w))
    probs, rest, out, inverse = forward(qkv_t, hot)

    dz = jnp.concatenate(
        [
            jnp.concatenate([quadrant(grad, False, False), from_col], axis=1),
            jnp.concatenate([from_row, from_both], axis=1),
        ],
        axis=0,
    ).reshape(tokens, width)

    r, c, d = lax.axis_size("row"), lax.axis_size("col"), lax.axis_size("dp")
    row, col, dp = lax.axis_index("row"), lax.axis_index("col"), lax.axis_index("dp")
    bit = core.astype(jnp.int32).reshape(1)
    dattn, wire, keep, gain = middle([out], w_proj, dz, norm_gain, bit, block_order(r, c))
    other = lax.ppermute(mine, "col", [(i, i ^ 1) for i in range(c)])
    norm = (tokens * r * c * d) ** (-0.5)
    got = lax.ppermute(wire, "col", [(i, i ^ 1) for i in range(c)])
    x, y, _ = position(row, col)

    def plane_round(pieces, turn):
        return [
            lax.ppermute(piece, ("row", "col"), plane_pairs(r, c, turn, n + 1))
            for n, piece in enumerate(pieces)
        ]

    def back_part(dattn, first, count):
        return backward(probs, rest, qkv_t, dattn, out, inverse, first, count)

    def halve(sums, gain, bit):
        index = dp // bit % 2
        (piece,), own, gain = round_pieces(sums, gain, index, 2)
        return piece, own, gain, index

    def swap(piece, bit):
        return lax.ppermute(piece, "dp", [(i, i ^ bit) for i in range(d)])

    first, second = groups // 4, groups // 4 + (groups - groups // 4) // 2
    part_a = back_part(dattn, 0, first)
    part_a, got = lax.optimization_barrier((part_a, got))
    sums = keep + got[GAIN_ROWS:].astype(F32)
    gain = gain + (got[0:1].astype(F32) + got[1:2].astype(F32))
    index = jnp.where(core == 0, x, y)
    pieces, own, gain = round_pieces(sums, gain, index, RADIX)
    dattn, pieces = lax.optimization_barrier((dattn, pieces))
    got = plane_round(pieces, 0)

    part_b = back_part(dattn, first, second - first)
    part_b, got = lax.optimization_barrier((part_b, got))
    sums, gain = round_sums(got, own, gain, index)
    index = jnp.where(core == 0, y, x)
    pieces, own, gain = round_pieces(sums, gain, index, RADIX)
    dattn, pieces = lax.optimization_barrier((dattn, pieces))
    got = plane_round(pieces, 1)

    part_c = back_part(dattn, second, groups - second)
    part_c, got = lax.optimization_barrier((part_c, got))
    sums, gain = round_sums(got, own, gain, index)
    piece, own, gain, index = halve(sums, gain, 4)
    part_c, piece = lax.optimization_barrier((part_c, piece))
    got = swap(piece, 4)

    parts = [part for trio in zip(part_a, part_b, part_c) for part in trio]
    quarters = back_product(parts, mine, other, bit)
    quarters, got = lax.optimization_barrier((quarters, got))
    local, to_col, to_row, to_both = [quarters[0]] + [
        shift(quarters[i], i // 2 == 1, i % 2 == 1, 1) for i in (1, 2, 3)
    ]
    sums, gain = round_sums([got], own, gain, index)
    piece, own, gain, index = halve(sums, gain, 2)
    sums, gain = round_sums([swap(piece, 2)], own, gain, index)
    sums, to_col = lax.optimization_barrier((sums, to_col))
    piece, own, gain, index = halve(sums, gain, 1)
    sums, gain = round_sums([swap(piece, 1)], own, gain, index)
    grad_proj, grad_gain = sums * norm, gain * norm
    grad_proj, grad_gain, to_row, to_both = lax.optimization_barrier(
        (grad_proj, grad_gain, to_row, to_both)
    )

    local, to_col, to_row, to_both = (
        part.reshape(square) for part in (local, to_col, to_row, to_both)
    )
    moved = jnp.concatenate(
        [
            jnp.concatenate([to_both, to_row], axis=1),
            jnp.concatenate([to_col, local], axis=1),
        ],
        axis=0,
    )
    grad_in = (grad.astype(F32) + moved.astype(F32)).astype(BF)[None]
    return (grad_in, grad_proj, grad_gain[0])


def solution(mesh):
    return jax.shard_map(
        per_device,
        mesh=mesh,
        in_specs=(
            P("dp", "row", "col", None),
            P("dp", "row", "col", None),
            P("dp", None),
            P(),
            P(),
            P("row", "col"),
        ),
        out_specs=(P("dp", "row", "col", None), P(("row", "col", "dp"), None), P()),
        check_vma=False,
    )
```

```python
import math

import jax
import jax.numpy as jnp
from jax import lax
from jax.experimental import pallas as pl
from jax.experimental.pallas import tpu as pltpu
from jax.sharding import PartitionSpec as P

HEADS = 32
GROUP = 4
BF = jnp.bfloat16
F32 = jnp.float32
NT = (((1,), (1,)), ((), ()))
TN = (((0,), (0,)), ((), ()))
LIMIT = 56 * 2**20
GAIN_ROWS = 8
RADIX = 4
REGIONS = 4


def params():
    return pltpu.CompilerParams(vmem_limit_bytes=LIMIT)


def shape(*dims):
    return lambda kind: jax.ShapeDtypeStruct(dims, kind)


def split3(value):
    high = value.astype(BF)
    rest = value - high.astype(F32)
    mid = rest.astype(BF)
    return high, mid, (rest - mid.astype(F32)).astype(BF)


def by_head(parts):
    return jnp.concatenate(parts, axis=0)


def zero_unless(chosen, value):
    return jnp.where(chosen, value, jnp.zeros_like(value))


def forward_kernel(q_ref, k_ref, v_ref, hot_ref, p_ref, rest_ref, o_ref, inv_ref):
    tokens, lanes = q_ref.shape
    size = lanes // GROUP
    main = p_ref.shape[2]
    tail = tokens - main
    factor = size ** (-0.5) * math.log2(math.e)
    queries, keys, values, hot = q_ref[...], k_ref[...], v_ref[...], hot_ref[...]
    lane = lax.broadcasted_iota(jnp.int32, (tokens, lanes), 1)
    head = lane // size
    mask = jnp.where(lane % size < REGIONS, (hot.astype(F32) - 1.0) * 1e30, 0.0).astype(BF)
    tail_keys, tail_values, tail_head = keys[main:], values[main:], head[:tail]
    tail_mask = zero_unless(tail_head == 0, mask[main:])
    tail_scores = lax.dot_general(
        jnp.concatenate([queries, hot], axis=1),
        jnp.concatenate(
            [
                by_head([zero_unless(tail_head == h, tail_keys) for h in range(GROUP)]),
                by_head([tail_mask] * GROUP),
            ],
            axis=1,
        ),
        NT,
        preferred_element_type=F32,
    )
    per = lanes // tail
    main_head = head[:main]

    def scores_of(h):
        left = jnp.where(head == h, queries, hot)
        right = jnp.where(main_head == h, keys[:main], mask[:main])
        return lax.dot_general(left, right, NT, preferred_element_type=F32)

    scores = scores_of(0)
    last, sums, tops = None, [], []
    for h in range(GROUP + 1):
        ahead = scores_of(h + 1) if h + 1 < GROUP else None
        if last is not None:
            own = main_head == h - 1
            summed = jnp.where(own, values[:main], jnp.ones_like(values[:main]))
            sums.append(jnp.dot(last, summed, preferred_element_type=F32))
        if h < GROUP:
            tile = tail_scores[:, lanes * (h // per) : lanes * (h // per + 1)]
            top = jnp.where(lane // tail == h % per, tile, -3e38)
            for start in range(0, main, lanes):
                top = jnp.maximum(top, scores[:, start : start + lanes])
            tops.append(jnp.max(top, axis=1, keepdims=True))
            last = jnp.exp2((scores - tops[h]) * factor).astype(BF)
            p_ref[h] = last
        scores = ahead
    rest = []
    for n in range(GROUP // per):
        top = tops[n * per]
        for i in range(1, per):
            top = jnp.where(lane // tail == i, tops[n * per + i], top)
        tile = tail_scores[:, lanes * n : lanes * (n + 1)]
        rest.append(jnp.exp2((tile - top) * factor).astype(BF))
    rest = jnp.concatenate(rest, axis=1)
    rest_ref[...] = rest
    ones = jnp.ones_like(tail_values)
    right = by_head(
        [
            jnp.concatenate(
                [zero_unless(tail_head == h, tail_values), zero_unless(tail_head == h, ones)], axis=1
            )
            for h in range(GROUP)
        ]
    )
    both = jnp.dot(rest, right, preferred_element_type=F32)
    out, total = None, None
    for h, part in enumerate(sums):
        turned = pltpu.roll(part, size, axis=1)
        out = part if out is None else jnp.where(head == h, part, out)
        total = turned if total is None else jnp.where(head == h, turned, total)
    inverse = 1.0 / (total + both[:, lanes:])
    o_ref[...] = (out + both[:, :lanes]) * inverse
    inv_ref[...] = inverse


def backward_kernel(
    p_ref, rest_ref, q_ref, k_ref, v_ref, do_ref, o_ref, inv_ref, dq_ref, dk_ref, dv_ref
):
    tokens, lanes = q_ref.shape
    size = lanes // GROUP
    main = p_ref.shape[2]
    tail = tokens - main
    scale = size ** (-0.5)
    keys, values, dout, inv = k_ref[...], v_ref[...], do_ref[...], inv_ref[...]
    lane = lax.broadcasted_iota(jnp.int32, (tokens, lanes), 1)
    head, which = lane // size, lane % size
    dout_f = dout.astype(F32)
    row_i = lax.broadcasted_iota(jnp.int32, (lanes, lanes), 0) // size
    col_i = lax.broadcasted_iota(jnp.int32, (lanes, lanes), 1)
    pick = jnp.where((col_i // size == (row_i + 1) % GROUP) & (col_i % size < 3), 1.0, 0.0).astype(BF)
    parts = jnp.concatenate(split3(dout_f * o_ref[...]), axis=1)
    delta = jnp.dot(parts, jnp.concatenate([pick] * 3, axis=0), preferred_element_type=F32)
    d_high = delta.astype(BF).astype(F32)
    d_rest = delta - d_high
    d_mid = d_rest.astype(BF).astype(F32)
    columns = jnp.where(
        which == 0, d_high, jnp.where(which == 1, d_mid, jnp.where(which == 2, d_rest - d_mid, 0.0))
    ).astype(BF)
    dout_t = (dout_f * inv).T.astype(BF)
    query_t = (q_ref[...].astype(F32) * (inv * scale)).T.astype(BF)
    tail_head, main_head = head[:tail], head[:main]

    def minus(h, count):
        chosen = (head[:count] == (h + 1) % GROUP) & (which[:count] < 3)
        return jnp.where(chosen, -1.0, 0.0).astype(BF)

    rest = rest_ref[...]
    right = by_head(
        [
            jnp.concatenate([zero_unless(tail_head == h, values[main:]), minus(h, tail)], axis=1)
            for h in range(GROUP)
        ]
    )
    dprobs = lax.dot_general(
        jnp.concatenate([dout, columns], axis=1), right, NT, preferred_element_type=F32
    )
    dscores_rest = (rest.astype(F32) * dprobs).astype(BF)

    def dprobs_of(h):
        left = jnp.where(head == h, dout, columns)
        right = jnp.where(main_head == h, values[:main], minus(h, main))
        return lax.dot_general(left, right, NT, preferred_element_type=F32)

    dprobs = dprobs_of(0)
    dq, dks, dvs = None, [], []
    for h in range(GROUP):
        ahead = dprobs_of(h + 1) if h + 1 < GROUP else None
        probs = p_ref[h]
        dscores = (probs.astype(F32) * dprobs).astype(BF)
        part = jnp.dot(dscores, keys[:main], preferred_element_type=F32)
        dq = part if dq is None else jnp.where(head == h, part, dq)
        rows = slice(size * h, size * (h + 1))
        dks.append(jnp.dot(query_t[rows], dscores, preferred_element_type=F32))
        dvs.append(jnp.dot(dout_t[rows], probs, preferred_element_type=F32))
        dprobs = ahead
    right = by_head([zero_unless(tail_head == h, keys[main:]) for h in range(GROUP)])
    dq = dq + jnp.dot(dscores_rest, right, preferred_element_type=F32)
    dq_ref[...] = (dq * (inv * scale)).astype(BF)
    for ref, whole, left, right in (
        (dk_ref, dks, query_t, dscores_rest),
        (dv_ref, dvs, dout_t, rest),
    ):
        ref[0:main] = jnp.concatenate(whole, axis=0).T.astype(BF)
        turned = jnp.dot(left, right, preferred_element_type=F32).T
        last = turned[0:tail]
        for h in range(1, GROUP):
            last = jnp.where(tail_head == h, turned[tail * h : tail * (h + 1)], last)
        ref[main:] = last.astype(BF)


def column_block(tokens, offset):
    return pl.BlockSpec((tokens, 128), lambda g: (0, g + offset))


def forward(qkv, hot):
    tokens = qkv.shape[0]
    per = qkv.shape[1] // 3 // 128
    main = tokens // 256 * 256
    rest = (tokens - main) * GROUP
    out = shape(tokens, per * 128)(F32)
    return pl.pallas_call(
        forward_kernel,
        grid=(per,),
        in_specs=[column_block(tokens, per * i) for i in range(3)]
        + [pl.BlockSpec((tokens, 128), lambda g: (0, 0))],
        out_specs=[
            pl.BlockSpec((GROUP, tokens, main), lambda g: (g, 0, 0)),
            pl.BlockSpec((tokens, rest), lambda g: (0, g)),
        ]
        + [column_block(tokens, 0)] * 2,
        out_shape=[
            shape(per * GROUP, tokens, main)(BF),
            shape(tokens, per * rest)(BF),
            out,
            out,
        ],
        compiler_params=params(),
        cost_estimate=pl.CostEstimate(
            flops=per * 3_200_000_000, bytes_accessed=per * 4_000_000, transcendentals=0
        ),
        name="attn_forward",
    )(qkv, qkv, qkv, hot)


def backward(probs, rest, qkv, dattn, out, inverse, first, count):
    tokens = qkv.shape[0]
    per = qkv.shape[1] // 3 // 128
    return pl.pallas_call(
        backward_kernel,
        grid=(count,),
        in_specs=[
            pl.BlockSpec((GROUP, *probs.shape[1:]), lambda g: (g + first, 0, 0)),
            pl.BlockSpec((tokens, rest.shape[1] // per), lambda g: (0, g + first)),
        ]
        + [column_block(tokens, first + per * i) for i in range(3)]
        + [column_block(tokens, first)] * 3,
        out_specs=[column_block(tokens, 0)] * 3,
        out_shape=[shape(tokens, count * 128)(BF)] * 3,
        compiler_params=params(),
        cost_estimate=pl.CostEstimate(
            flops=count * 3_600_000_000, bytes_accessed=count * 4_000_000, transcendentals=0
        ),
        name="attn_backward",
    )(probs, rest, qkv, qkv, qkv, dattn, out, inverse)


def pack_gain(high, low):
    rows = lax.broadcasted_iota(jnp.int32, (GAIN_ROWS, high.shape[1]), 0)
    return jnp.where(rows == 0, high, jnp.where(rows == 1, low, 0.0)).astype(BF)


def middle_kernel(order, bit_ref, *refs):
    outs, (w_ref, dz_ref, gain_ref, do_ref, send_ref, keep_ref, term_ref, sums) = refs[:-8], refs[-8:]
    attn = jnp.concatenate([ref[...].astype(BF) for ref in outs], axis=1)
    weights = w_ref[...]
    proj = jnp.dot(attn, weights, preferred_element_type=F32)
    centred = proj - jnp.mean(proj, axis=1, keepdims=True)
    rstd = lax.rsqrt(jnp.mean(centred * centred, axis=1, keepdims=True) + 1e-05)
    normed = centred * rstd
    dz = dz_ref[...].astype(F32)
    term = jnp.sum(dz * normed, axis=0, keepdims=True)
    scaled = dz * gain_ref[...]
    mean = jnp.mean(scaled, axis=1, keepdims=True)
    dot = jnp.mean(scaled * normed, axis=1, keepdims=True)
    dproj = (rstd * (scaled - mean - normed * dot)).astype(BF)
    do_ref[...] = lax.dot_general(dproj, weights, NT, preferred_element_type=F32).astype(BF)
    sums[...] = lax.dot_general(attn, dproj, TN, preferred_element_type=F32)
    half = len(order) // 2
    size = sums.shape[0] // len(order)
    low, high = (
        jnp.concatenate([sums[size * b : size * (b + 1)] for b in part], axis=0)
        for part in (order[:half], order[half:])
    )
    second = bit_ref[0] == 1
    term_high = term.astype(BF).astype(F32)
    term_low = (term - term_high).astype(BF).astype(F32)
    send_ref[0:GAIN_ROWS] = pack_gain(term_high, term_low)
    send_ref[GAIN_ROWS:] = jnp.where(second, low, high).astype(BF)
    keep_ref[...] = jnp.where(second, high, low)
    term_ref[...] = term_high + term_low


def middle(outs, w_proj, dz, gain, bit, order):
    tokens, width = dz.shape
    vmem = pl.BlockSpec(memory_space=pltpu.VMEM)
    half = width // 2
    return pl.pallas_call(
        lambda *refs: middle_kernel(order, *refs),
        in_specs=[pl.BlockSpec(memory_space=pltpu.SMEM)] + [vmem] * (len(outs) + 3),
        out_specs=[vmem] * 4,
        out_shape=[
            shape(tokens, width)(BF),
            shape(GAIN_ROWS + half, width)(BF),
            shape(half, width)(F32),
            shape(1, width)(F32),
        ],
        scratch_shapes=[pltpu.VMEM((width, width), F32)],
        compiler_params=params(),
        cost_estimate=pl.CostEstimate(
            flops=8_000_000_000, bytes_accessed=16_000_000, transcendentals=0
        ),
        name="middle",
    )(bit, *outs, w_proj, dz, gain[None])


def back_kernel(core_ref, *refs):
    parts, (mine_ref, other_ref), outs = refs[:-6], refs[-6:-4], refs[-4:]
    first = core_ref[0] == 0
    left = jnp.concatenate([ref[...] for ref in parts], axis=1)
    rows = 64
    blocks = []
    for z in range(mine_ref.shape[0] // rows):
        mine, other = mine_ref[rows * z : rows * (z + 1)], other_ref[rows * z : rows * (z + 1)]
        blocks += [jnp.where(first, mine, other), jnp.where(first, other, mine)]
    total = lax.dot_general(left, jnp.concatenate(blocks, axis=0), NT, preferred_element_type=F32)
    side = math.isqrt(total.shape[0])
    half = side // 2
    for n, ref in enumerate(outs):
        start = side * half * (n // 2) + half * (n % 2)
        ref[...] = jnp.concatenate(
            [total[start + side * i : start + side * i + half] for i in range(half)], axis=0
        ).astype(BF)


def back_product(parts, mine, other, core):
    tokens = parts[0].shape[0]
    rows, inner = mine.shape
    steps = 4
    wide = 2 * rows // steps
    side = pl.BlockSpec((rows // steps, inner), lambda g: (g, 0))
    out = pl.BlockSpec((tokens // 4, wide), lambda g: (0, g))
    return pl.pallas_call(
        back_kernel,
        grid=(steps,),
        in_specs=[pl.BlockSpec(memory_space=pltpu.SMEM)]
        + [pl.BlockSpec(part.shape, lambda g: (0, 0)) for part in parts]
        + [side] * 2,
        out_specs=[out] * 4,
        out_shape=[shape(tokens // 4, wide * steps)(BF)] * 4,
        compiler_params=params(),
        cost_estimate=pl.CostEstimate(
            flops=6_000_000_000, bytes_accessed=12_000_000, transcendentals=0
        ),
        name="back_product",
    )(core, *parts, mine, other)


def position(row, col):
    return row // 2, row % 2 * 2 + col // 2, col % 2


def place(x, y, core):
    return x * 2 + y // 2, y % 2 * 2 + core


def block_order(row_count, col_count):
    order = []
    for core in range(2):
        for first in range(RADIX):
            for second in range(RADIX):
                x, y = (first, second) if core == 0 else (second, first)
                row, col = place(x, y, core)
                order.append(row * col_count + col)
    return order


def plane_pairs(rows, cols, turn, step):
    pairs = []
    for r in range(rows):
        for c in range(cols):
            x, y, core = position(r, c)
            if core == turn:
                x = (x + step) % RADIX
            else:
                y = (y + step) % RADIX
            to_r, to_c = place(x, y, core)
            pairs.append((r * cols + c, to_r * cols + to_c))
    return pairs


def round_pieces(total, gain, index, count):
    rows = total.shape[0] // count
    high = lax.reduce_precision(gain, 8, 7)
    low = lax.reduce_precision(gain - high, 8, 7)
    packed = pack_gain(high, low)
    pieces = [
        jnp.concatenate(
            [
                packed,
                lax.dynamic_slice_in_dim(total, (index + n) % count * rows, rows, 0).astype(BF),
            ],
            axis=0,
        )
        for n in range(1, count)
    ]
    return pieces, lax.dynamic_slice_in_dim(total, index * rows, rows, 0), high + low


def round_sums(got, own, gain, index):
    count = len(got) + 1
    gains = [gain]
    for value in got:
        own = own + value[GAIN_ROWS:].astype(F32)
        gains.append(value[0:1].astype(F32) + value[1:2].astype(F32))
    if count == 2:
        return own, gains[0] + gains[1]
    turned = jnp.concatenate(gains[::-1] * 2, axis=0)
    ordered = lax.dynamic_slice_in_dim(turned, count - 1 - index, count, 0)
    gain = ordered[0:1]
    for n in range(1, count):
        gain = gain + ordered[n : n + 1]
    return own, gain


def shift(value, rows, cols, step):
    r, c = lax.axis_size("row"), lax.axis_size("col")
    if rows and cols:
        pairs = [
            (i * c + j, (i + step) % r * c + (j + step) % c) for i in range(r) for j in range(c)
        ]
        return lax.ppermute(value, ("row", "col"), pairs)
    name, count = ("row", r) if rows else ("col", c)
    return lax.ppermute(value, name, [(i, (i + step) % count) for i in range(count)])


def quadrant(values, low_row, low_col):
    half = values.shape[0] // 2
    rows = slice(0, half) if low_row else slice(half, None)
    cols = slice(0, half) if low_col else slice(half, None)
    return values[rows, cols]


def per_device(qkv, grad_out, w_qkv, w_proj, norm_gain, region):
    side, width = grad_out.shape[1], grad_out.shape[3]
    half = side // 2
    tokens = side * side
    grad = grad_out[0]
    flat = (half * half, width)
    square = (half, half, width)

    def send(value, rows, cols, step):
        return shift(value.reshape(flat), rows, cols, step).reshape(square)

    core = lax.axis_index("col") % 2
    rows = w_qkv.shape[0] // 2
    mine_w = lax.dynamic_slice_in_dim(w_qkv, core * rows, rows, 0)
    mine = lax.all_gather(mine_w, "dp", axis=0, tiled=True)
    from_row = send(quadrant(grad, True, False), True, False, -1)
    from_col = send(quadrant(grad, False, True), False, True, -1)
    from_both = send(quadrant(grad, True, True), True, True, -1)

    ids = region.reshape(tokens, 1)
    lane = lax.broadcasted_iota(jnp.int32, (tokens, 128), 1)
    hot = (ids == lane % (width // HEADS)).astype(BF)
    qkv_t = qkv.reshape(tokens, 3 * width)
    groups = width // 128
    qkv_t, mine_w = lax.optimization_barrier((qkv_t, mine_w))
    probs, rest, out, inverse = forward(qkv_t, hot)

    dz = jnp.concatenate(
        [
            jnp.concatenate([quadrant(grad, False, False), from_col], axis=1),
            jnp.concatenate([from_row, from_both], axis=1),
        ],
        axis=0,
    ).reshape(tokens, width)

    r, c, d = lax.axis_size("row"), lax.axis_size("col"), lax.axis_size("dp")
    row, col, dp = lax.axis_index("row"), lax.axis_index("col"), lax.axis_index("dp")
    bit = core.astype(jnp.int32).reshape(1)
    dattn, wire, keep, gain = middle([out], w_proj, dz, norm_gain, bit, block_order(r, c))
    other = lax.ppermute(mine, "col", [(i, i ^ 1) for i in range(c)])
    norm = (tokens * r * c * d) ** (-0.5)
    got = lax.ppermute(wire, "col", [(i, i ^ 1) for i in range(c)])
    x, y, _ = position(row, col)

    def plane_round(pieces, turn):
        return [
            lax.ppermute(piece, ("row", "col"), plane_pairs(r, c, turn, n + 1))
            for n, piece in enumerate(pieces)
        ]

    def back_part(dattn, first, count):
        return backward(probs, rest, qkv_t, dattn, out, inverse, first, count)

    def halve(sums, gain, bit):
        index = dp // bit % 2
        (piece,), own, gain = round_pieces(sums, gain, index, 2)
        return piece, own, gain, index

    def swap(piece, bit):
        return lax.ppermute(piece, "dp", [(i, i ^ bit) for i in range(d)])

    first, second = groups // 4, groups // 4 + (groups - groups // 4) // 2
    part_a = back_part(dattn, 0, first)
    part_a, got = lax.optimization_barrier((part_a, got))
    sums = keep + got[GAIN_ROWS:].astype(F32)
    gain = gain + (got[0:1].astype(F32) + got[1:2].astype(F32))
    index = jnp.where(core == 0, x, y)
    pieces, own, gain = round_pieces(sums, gain, index, RADIX)
    dattn, pieces = lax.optimization_barrier((dattn, pieces))
    got = plane_round(pieces, 0)

    part_b = back_part(dattn, first, second - first)
    part_b, got = lax.optimization_barrier((part_b, got))
    sums, gain = round_sums(got, own, gain, index)
    index = jnp.where(core == 0, y, x)
    pieces, own, gain = round_pieces(sums, gain, index, RADIX)
    dattn, pieces = lax.optimization_barrier((dattn, pieces))
    got = plane_round(pieces, 1)

    part_c = back_part(dattn, second, groups - second)
    part_c, got = lax.optimization_barrier((part_c, got))
    sums, gain = round_sums(got, own, gain, index)
    piece, own, gain, index = halve(sums, gain, 4)
    part_c, piece = lax.optimization_barrier((part_c, piece))
    got = swap(piece, 4)

    parts = [part for trio in zip(part_a, part_b, part_c) for part in trio]
    quarters = back_product(parts, mine, other, bit)
    quarters, got = lax.optimization_barrier((quarters, got))
    local, to_col, to_row, to_both = [quarters[0]] + [
        shift(quarters[i], i // 2 == 1, i % 2 == 1, 1) for i in (1, 2, 3)
    ]
    sums, gain = round_sums([got], own, gain, index)
    piece, own, gain, index = halve(sums, gain, 2)
    sums, gain = round_sums([swap(piece, 2)], own, gain, index)
    sums, to_col = lax.optimization_barrier((sums, to_col))
    piece, own, gain, index = halve(sums, gain, 1)
    sums, gain = round_sums([swap(piece, 1)], own, gain, index)
    grad_proj, grad_gain = sums * norm, gain * norm
    grad, grad_proj, grad_gain = lax.optimization_barrier((grad, grad_proj, grad_gain))

    local, to_col, to_row, to_both = (
        part.reshape(square) for part in (local, to_col, to_row, to_both)
    )
    moved = jnp.concatenate(
        [
            jnp.concatenate([to_both, to_row], axis=1),
            jnp.concatenate([to_col, local], axis=1),
        ],
        axis=0,
    )
    grad_in = (grad.astype(F32) + moved.astype(F32)).astype(BF)[None]
    return (grad_in, grad_proj, grad_gain[0])


def solution(mesh):
    return jax.shard_map(
        per_device,
        mesh=mesh,
        in_specs=(
            P("dp", "row", "col", None),
            P("dp", "row", "col", None),
            P("dp", None),
            P(),
            P(),
            P("row", "col"),
        ),
        out_specs=(P("dp", "row", "col", None), P(("row", "col", "dp"), None), P()),
        check_vma=False,
    )
```
